128 devices in a mesh: ctx: 16 (over y, x_hi, core), tp: 8 (over x_lo, z).
Axes of the slice: x: 4 (x_hi: 2, x_lo: 2; x = x_hi * 2 + x_lo), y: 4, z: 4, core: 2. Of those that a mesh axis runs over, the one named last changes fastest.
Arguments:
- query_proj: bfloat16 [16384, 8192], P('ctx', 'tp'), may hold values from -6 to 6
- key_proj: bfloat16 [16384, 8192], P('ctx', 'tp'), may hold values from -6 to 6
- value_proj: bfloat16 [16384, 8192], P('ctx', 'tp'), may hold values from -6 to 6
- cotangent: bfloat16 [16384, 8192], P('ctx', 'tp'), may hold values from -6 to 6
- short_taps: float32 [3, 3, 8192], P(None, None, 'tp'), may hold values from -2.5 to 2.5
- residues: float32 [512, 16], P('tp'), may hold values from -0.6 to 0.6
- decay_rates: float32 [512, 16], P('tp'), may hold values from 1.8310548e-05 to 0.08
Outputs:
- mixed: bfloat16 [16384, 8192], P('ctx', 'tp')
- grad_query: bfloat16 [16384, 8192], P('ctx', 'tp')
- grad_key: bfloat16 [16384, 8192], P('ctx', 'tp')
- grad_value: bfloat16 [16384, 8192], P('ctx', 'tp')
- grad_taps: float32 [3, 3, 8192], P(None, None, 'tp')
- grad_residues: float32 [512, 16], P('tp')
The draws below stay inside these ranges and needn't reach their ends.
All inputs are finite; a program needn't handle non-finite values.
Results may differ from the reference program's by a relative error of at most 0.014.
Values may be sent and summed in bfloat16 or wider, within the bound.
A program may use at most 128 MiB of HBM per device.

```python
import math
import jax
import jax.numpy as jnp
from jax import lax

D = 8192
TAPS = 3
MODES = 16
FILTER_GROUPS = 512
SEQ = 16384


def level_of(stream_key, shape, split, smallest, largest):
    loudness, own = 1.0, jax.random.fold_in(stream_key, 6)
    for position, parts in split:
        steps = jnp.exp(jax.random.uniform(jax.random.fold_in(own, position), (parts,), jnp.float32, smallest / len(split), largest / len(split)))
        loudness = loudness * jnp.repeat(steps, shape[position] // parts).reshape([-1 if axis == position else 1 for axis in range(len(shape))])
    return loudness


def scatter_about(stream_key, extent, scale, limit, pieces=(), kind=jnp.bfloat16):
    array = scale * jax.random.normal(stream_key, extent, jnp.float32)
    if pieces:
        array = array * level_of(stream_key, extent, pieces, -0.22, 0.18)
    return jnp.clip(array, -limit, limit).astype(kind)


def setup_inputs(seed: int = 0) -> dict:
    key_list = jax.random.split(jax.random.key(seed), 8)
    return {
        "query_proj": scatter_about(key_list[0], (SEQ, D), 1.0, 6.0, ((0, 16), (1, 8))),
        "key_proj": scatter_about(key_list[1], (SEQ, D), 1.0, 6.0, ((0, 16), (1, 8))),
        "value_proj": scatter_about(key_list[2], (SEQ, D), 1.0, 6.0, ((0, 16), (1, 8))),
        "cotangent": scatter_about(key_list[3], (SEQ, D), 1.0, 6.0, ((0, 16), (1, 8))),
        "short_taps": scatter_about(key_list[4], (3, TAPS, D), 0.6, 2.5, ((2, 8),), jnp.float32),
        "residues": scatter_about(key_list[5], (FILTER_GROUPS, MODES), 0.1, 0.6, ((0, 8),), jnp.float32),
        "decay_rates": jnp.clip(jnp.exp(math.log(0.08) - 8.3823046 * jax.random.uniform(key_list[6], (FILTER_GROUPS, MODES), jnp.float32) ** level_of(key_list[6], (FILTER_GROUPS, MODES), ((0, 8),), -0.2, 0.2)), 1.831054760259576e-05, 0.08),
    }


def kernel_tables(residues, decay_rates, block_len):
    offsets = jnp.arange(block_len, dtype=jnp.float32)
    spread = offsets[:, None] - offsets[None, :]
    causal = spread >= 0.0
    lagged = jnp.maximum(spread, 0.0)
    toeplitz = jnp.zeros((residues.shape[0], block_len, block_len), jnp.float32)
    for mode_index in range(residues.shape[1]):
        rate = decay_rates[:, mode_index][:, None, None]
        toeplitz = toeplitz + residues[:, mode_index][:, None, None] * jnp.exp(-rate * lagged[None])
    toeplitz = jnp.where(causal[None], toeplitz, jnp.zeros_like(toeplitz))
    readin = residues[:, :, None] * jnp.exp(-decay_rates[:, :, None] * (offsets + 1.0)[None, None, :])
    absorb = jnp.exp(-decay_rates[:, :, None] * (block_len - 1.0 - offsets)[None, None, :])
    passing = jnp.exp(-decay_rates * block_len)
    return (toeplitz, readin, absorb, passing)

def state_combine(earlier, later):
    return (earlier[0] * later[0], later[1] + later[0] * earlier[1])

def modal_conv(columns, residues, decay_rates):
    width, length = columns.shape
    groups, modes = residues.shape
    members = width // groups
    block_len = min(128, length)
    count = length // block_len
    toeplitz, readin, absorb, passing = kernel_tables(residues, decay_rates, block_len)
    blocks = columns.reshape(groups, members, count, block_len)
    inner = jnp.einsum('gts,gkns->gknt', toeplitz, blocks, precision=lax.Precision.HIGHEST)
    ends = jnp.einsum('gms,gkns->nmgk', absorb, blocks, precision=lax.Precision.HIGHEST).reshape(count, modes, width)
    rate_columns = jnp.repeat(passing.T, members, axis=1)
    factors = jnp.broadcast_to(rate_columns[None], (count, modes, width))
    after_block = lax.associative_scan(state_combine, (factors, ends), axis=0)[1]
    before = jnp.concatenate([jnp.zeros((1, modes, width), jnp.float32), after_block[:-1]], axis=0)
    carried = jnp.einsum('gmt,nmgk->gknt', readin, before.reshape(count, modes, groups, members), precision=lax.Precision.HIGHEST)
    return ((inner + carried).reshape(width, length), after_block[-1])

def short_forward(stream, prior, taps):
    span = taps.shape[0] - 1
    length = stream.shape[0]
    extended = jnp.concatenate([prior, stream], axis=0)
    total = jnp.zeros(stream.shape, jnp.float32)
    for lag_index in range(taps.shape[0]):
        window = extended[span - lag_index:span - lag_index + length].astype(jnp.float32)
        total = total + taps[lag_index][None, :] * window
    return total

def short_backward(grad_out, after, stream, prior, taps):
    span = taps.shape[0] - 1
    length = stream.shape[0]
    extended = jnp.concatenate([prior, stream], axis=0)
    extended_grad = jnp.concatenate([grad_out, after], axis=0)
    grad_in = jnp.zeros(grad_out.shape, jnp.float32)
    tap_rows = []
    for lag_index in range(taps.shape[0]):
        grad_in = grad_in + taps[lag_index][None, :] * extended_grad[lag_index:lag_index + length]
        window = extended[span - lag_index:span - lag_index + length].astype(jnp.float32)
        tap_rows.append(lax.optimization_barrier(jnp.sum(grad_out * window, axis=0)))
    return (grad_in, jnp.stack(tap_rows))

def reference(query_proj, key_proj, value_proj, cotangent, short_taps, residues, decay_rates):
    span = TAPS - 1
    prior = jnp.zeros((span, D), jnp.bfloat16)
    after = jnp.zeros((span, D), jnp.float32)
    query_short = short_forward(query_proj, prior, short_taps[0])
    key_short = short_forward(key_proj, prior, short_taps[1])
    value_short = short_forward(value_proj, prior, short_taps[2])
    gated_low = (key_short * value_short).astype(jnp.bfloat16)
    gated_cols = lax.optimization_barrier(gated_low.T).astype(jnp.float32)
    outputs, unwind = jax.vjp(lambda signal, weights: modal_conv(signal, weights, decay_rates), gated_cols, residues)
    long_cols, final = outputs
    long_low = long_cols.T.astype(jnp.bfloat16)
    long_out = lax.optimization_barrier(long_low).astype(jnp.float32)
    mixed = (query_short * long_out).astype(jnp.bfloat16)
    grad_cot = cotangent.astype(jnp.float32)
    grad_qshort = grad_cot * long_out
    grad_long_low = (grad_cot * query_short).astype(jnp.bfloat16)
    grad_long_cols = lax.optimization_barrier(grad_long_low.T).astype(jnp.float32)
    grad_gated_cols, grad_residues = unwind((grad_long_cols, jnp.zeros_like(final)))
    grad_gated_low = grad_gated_cols.T.astype(jnp.bfloat16)
    grad_gated = lax.optimization_barrier(grad_gated_low).astype(jnp.float32)
    grad_kshort = grad_gated * value_short
    grad_vshort = grad_gated * key_short
    grad_query, taps_query = short_backward(grad_qshort, after, query_proj, prior, short_taps[0])
    grad_key, taps_key = short_backward(grad_kshort, after, key_proj, prior, short_taps[1])
    grad_value, taps_value = short_backward(grad_vshort, after, value_proj, prior, short_taps[2])
    grad_taps = jnp.stack([taps_query, taps_key, taps_value])
    return (mixed, grad_query.astype(jnp.bfloat16), grad_key.astype(jnp.bfloat16), grad_value.astype(jnp.bfloat16), grad_taps, grad_residues)
```

```python
import functools

import jax
import jax.numpy as jnp
from jax import lax
from jax.experimental import pallas as pl
from jax.experimental.pallas import tpu as pltpu
from jax.sharding import PartitionSpec as P

BLK = 128
LANES = 128
MEM = 16
HI = lax.Precision.HIGHEST
F32 = jnp.float32
BF16 = jnp.bfloat16
MESH = pl.DeviceIdType.MESH


def lane_iota(rows):
    return lax.broadcasted_iota(jnp.int32, (rows, LANES), 1)


def row_iota(rows):
    return lax.broadcasted_iota(jnp.int32, (rows, LANES), 0)


def swap8(parts):
    piece = lane_iota(parts[0].shape[0]) // MEM
    for d in (4, 2, 1):
        high = (piece // d) % 2 == 1
        swapped = list(parts)
        for a in range(8):
            if a & d:
                continue
            low_part, high_part = parts[a], parts[a + d]
            swapped[a] = jnp.where(high, pltpu.roll(high_part, MEM * d, 1), low_part)
            swapped[a + d] = jnp.where(high, high_part, pltpu.roll(low_part, LANES - MEM * d, 1))
        parts = swapped
    return parts


def split(value):
    high = value.astype(BF16)
    low = (value - high.astype(F32)).astype(BF16)
    return high, low


def dot(a, b, dims=((1,), (0,))):
    return lax.dot_general(a, b, (dims, ((), ())), preferred_element_type=F32)


def column(table, g):
    return jnp.broadcast_to(table[:, MEM * g : MEM * g + 1], table.shape)


def kernel(
    n, tiles, halves, length, modes,
    query, key, value, cot, taps, rates, weights,
    mixed, grad_q, grad_k, grad_v, taps_out, res_out,
    inb, uf, ef, x3, g3, tf, tb, yv, zv, fs, gb, st, rs, halo, after, rn, wn, r3, w3, sout, gin,
    stage, tsum, trecv, gacc, grecv,
    in_sem, hs_sem, hr_sem, ss_sem, sr_sem, out_sem, ts_sem, tr_sem, gs_sem, gr_sem,
):
    me = lax.axis_index("ctx")
    blocks = length // BLK
    per = tiles // halves
    barrier = pltpu.get_barrier_semaphore()
    for d in range(1, n):
        pl.semaphore_signal(barrier, inc=1, device_id={"ctx": lax.rem(me + d, n)}, device_id_type=MESH)

    streams = (query, key, value, cot)

    def fetch(i, j):
        return pltpu.make_async_copy(
            streams[i].at[:, pl.ds(pl.multiple_of(j * LANES, LANES), LANES)], inb.at[i, j], in_sem.at[i, j]
        )

    for j in range(tiles):
        for i in range(4):
            fetch(i, j).start()

    group8 = (lane_iota(8) // MEM == row_iota(8)).astype(F32)
    repeat = (lane_iota(modes) % modes == row_iota(modes)).astype(F32)
    for j in range(tiles):
        rows = pl.ds(8 * j, 8)
        rn[j] = lax.dot_general(rates[rows, :], group8, (((0,), (0,)), ((), ())), precision=HI, preferred_element_type=F32)
        wn[j] = lax.dot_general(weights[rows, :], group8, (((0,), (0,)), ((), ())), precision=HI, preferred_element_type=F32)
    r3[...] = lax.dot_general(rates[...], repeat, (((1,), (0,)), ((), ())), precision=HI, preferred_element_type=F32)
    w3[...] = lax.dot_general(weights[...], repeat, (((1,), (0,)), ((), ())), precision=HI, preferred_element_type=F32)

    pl.semaphore_wait(barrier, n - 1)

    def behind(i):
        return pltpu.make_async_remote_copy(
            src_ref=streams[i].at[pl.ds(length - 16, 16), :], dst_ref=halo.at[i],
            send_sem=hs_sem.at[i], recv_sem=hr_sem.at[i],
            device_id={"ctx": lax.rem(me + 1, n)}, device_id_type=MESH,
        )

    def ahead(i):
        return pltpu.make_async_remote_copy(
            src_ref=streams[i].at[pl.ds(0, 16), :], dst_ref=after.at[i],
            send_sem=hs_sem.at[3 + i], recv_sem=hr_sem.at[3 + i],
            device_id={"ctx": lax.rem(me + n - 1, n)}, device_id_type=MESH,
        )

    for i in range(3):
        behind(i).start()
    for i in range(4):
        ahead(i).start()

    t_row = row_iota(BLK).astype(F32)
    lane_f = lane_iota(modes).astype(F32)
    lane_b = lane_iota(BLK)
    causal = row_iota(BLK) >= lane_iota(BLK)
    anti = row_iota(BLK) <= lane_iota(BLK)

    def build(j, _):
        rn_j = rn[j]
        for g in range(8):
            at = 8 * j + g
            r_row = r3[pl.ds(at, 1), :]
            w_row = w3[pl.ds(at, 1), :]
            r_col = column(rn_j, g)
            pad = jnp.zeros((LANES - 3 * modes, LANES), BF16)
            for ref, reach, peer, mask in (
                (tf, t_row + 1.0, lane_f + 1.0, causal),
                (tb, (BLK - 1.0) - t_row, (BLK - 1.0) - lane_f, anti),
            ):
                high, low = split(w_row * jnp.exp(-r_row * reach))
                zero = jnp.zeros_like(high)
                left = jnp.where(lane_b < 2 * modes, high, jnp.where(lane_b < 3 * modes, low, zero))
                v_high, v_low = split(jnp.exp(r_col * peer))
                right = jnp.concatenate([v_high, v_low, v_high, pad], axis=0)
                table = dot(left, right)
                ref[at, :, 0:BLK] = jnp.where(mask, table, 0.0).astype(BF16)
                ref[at, :, BLK : 2 * BLK] = left
        return 0

    lax.fori_loop(0, tiles, build, 0)

    for i in range(3):
        behind(i).wait()
    for i in range(4):
        ahead(i).wait()

    first = (me == 0)
    last = (me == n - 1)
    lane16 = lane_iota(modes)
    piece16 = lane16 // MEM

    def phase1(j, _):
        lanes = pl.ds(pl.multiple_of(j * LANES, LANES), LANES)
        for i in range(4):
            fetch(i, j).wait()
        for i in range(3):
            prior = halo[i, :, lanes].astype(F32)[8:16]
            uf[j, i, 0:8, :] = jnp.where(first, 0.0, prior)
            nxt = after[i, :, lanes].astype(F32)[0:8]
            uf[j, i, 8 + length : 16 + length, :] = jnp.where(last, 0.0, nxt)

        def widen(c, _):
            for i in range(3):
                rows = pl.ds(pl.multiple_of(c * 64, 64), 64)
                uf[j, i, pl.ds(pl.multiple_of(c * 64 + 8, 8), 64), :] = inb[i, j, rows, :].astype(F32)
            return 0

        lax.fori_loop(0, length // 64, widen, 0)
        tap = [[taps[i, l : l + 1, lanes] for l in range(3)] for i in range(3)]

        def gate(c, _):
            s0 = pl.multiple_of(c * 16, 16)
            xs, gs = [], []
            for b in range(8):
                base = pl.multiple_of(b * BLK + s0, 16)
                short = []
                for i in range(3):
                    view = uf.at[j, i, pl.ds(base, 24), :]
                    total = tap[i][0] * view[8:24, :] + tap[i][1] * view[7:23, :] + tap[i][2] * view[6:22, :]
                    short.append(total)
                xs.append(short[1] * short[2])
                gs.append(inb[3, j, pl.ds(base, 16), :].astype(F32) * short[0])
            for ref, parts in ((x3, xs), (g3, gs)):
                for g, part in enumerate(swap8(parts)):
                    ref[8 * j + g, pl.ds(s0, 16), :] = part.astype(BF16)
            return 0

        lax.fori_loop(0, BLK // 16, gate, 0)

        rn_j = rn[j]
        ahead_state = jnp.zeros((modes, LANES), F32)
        back_state = jnp.zeros((modes, LANES), F32)
        for g in range(8):
            at = 8 * j + g
            r_col = column(rn_j, g)
            absorb = jnp.concatenate(split(jnp.exp(-r_col * ((BLK - 1.0) - lane_f))), axis=0)
            ends2 = dot(absorb, x3[at, 0:BLK, :])
            ends = ends2[0:modes] + ends2[modes : 2 * modes]
            emit = jnp.concatenate(split(jnp.exp(-r_col * (lane_f + 1.0))), axis=0)
            starts2 = dot(emit, g3[at, 0:BLK, :])
            starts = starts2[0:modes] + starts2[modes : 2 * modes]
            gb[at] = starts
            power = jnp.exp(-r_col * float(BLK))
            for d in (1, 2, 4):
                moved = pltpu.roll(ends, MEM * d, 1)
                ends = ends + jnp.where(piece16 >= d, power * moved, 0.0)
                moved = pltpu.roll(starts, LANES - MEM * d, 1)
                starts = starts + jnp.where(piece16 < 8 - d, power * moved, 0.0)
                power = power * power
            ends_next = pltpu.roll(ends, MEM, 1)
            starts_prev = pltpu.roll(starts, LANES - MEM, 1)
            fs[0, at] = jnp.where(piece16 == 0, 0.0, ends_next)
            fs[1, at] = jnp.where(piece16 == 7, 0.0, starts_prev)
            place = pltpu.roll(ends_next, MEM * g, 1) if g else ends_next
            ahead_state = jnp.where(piece16 == g, place, ahead_state)
            place = pltpu.roll(starts, MEM * g, 1) if g else starts
            back_state = jnp.where(piece16 == g, place, back_state)
        st[j // per, 0, j % per] = ahead_state
        st[j // per, 1, j % per] = back_state
        return 0

    def send(h, d):
        return pltpu.make_async_remote_copy(
            src_ref=st.at[h, (me + d) // n], dst_ref=rs.at[h, d],
            send_sem=ss_sem.at[h, d], recv_sem=sr_sem.at[h, d],
            device_id={"ctx": lax.rem(me + d, n)}, device_id_type=MESH,
        )

    for h in range(halves):
        lax.fori_loop(h * per, (h + 1) * per, phase1, 0)
        for d in range(1, n):
            send(h, d).start()

    gacc[...] = jnp.zeros_like(gacc)

    def within(j, _):
        rn_j = rn[j]
        total = gacc[...]
        for g in range(8):
            at = 8 * j + g
            r_col = column(rn_j, g)
            pairs = dot(x3[at, 0:BLK, :], g3[at, 0:BLK, :], ((1,), (1,)))
            pairs = jnp.where(anti, pairs, 0.0).astype(BF16)
            rise = jnp.concatenate(split(jnp.exp(r_col * lane_f)), axis=0)
            both = dot(rise, pairs)
            terms = (both[0:modes] + both[modes : 2 * modes]) * jnp.exp(-r_col * lane_f)
            total = jnp.where(lane16 == at, total + jnp.sum(terms, axis=1, keepdims=True), total)
        gacc[...] = total
        return 0

    lax.fori_loop(0, tiles, within, 0)

    def combine(j, h):
        jj = j - h * per
        rn_j = rn[j]
        whole = jnp.exp(-rn_j * float(length))
        into = jnp.zeros((modes, LANES), F32)
        back = jnp.zeros((modes, LANES), F32)
        for e in range(n - 1, 0, -1):
            into = whole * into + jnp.where(e <= me, rs[h, e, jj], 0.0)
            back = whole * back + jnp.where(e <= n - 1 - me, rs[h, n - e, jj], 0.0)
        sout[j] = whole * into + st[h, 0, jj]
        gin[j] = back
        total = gacc[...]
        zeros = jnp.zeros((2 * BLK - BLK - 3 * modes, LANES), BF16)
        for g in range(8):
            at = 8 * j + g
            r_col = column(rn_j, g)
            here = []
            for state in (into, back):
                spread = jnp.where(piece16 == g, state, 0.0)
                for d in (1, 2, 4):
                    spread = spread + pltpu.roll(spread, MEM * d, 1)
                here.append(spread)
            step = piece16.astype(F32) * float(BLK)
            before = fs[0, at] + jnp.exp(-r_col * step) * here[0]
            behind_ = fs[1, at] + jnp.exp(-r_col * ((7.0 * BLK) - step)) * here[1]
            total = jnp.where(lane16 == at, total + jnp.sum(gb[at] * before, axis=1, keepdims=True), total)
            for ref, state in ((x3, before), (g3, behind_)):
                high, low = split(state)
                ref[at, BLK : 2 * BLK, :] = jnp.concatenate([high, low, high, zeros], axis=0)
        gacc[...] = total
        return h

    def put(i, j, slot):
        return pltpu.make_async_copy(
            stage.at[slot, i], (mixed, grad_q, grad_k, grad_v)[i].at[:, pl.ds(pl.multiple_of(j * LANES, LANES), LANES)],
            out_sem.at[slot, i],
        )

    def phase2(j, _):
        lanes = pl.ds(pl.multiple_of(j * LANES, LANES), LANES)
        slot = j % 2

        @pl.when(j >= 2)
        def _():
            for i in range(4):
                put(i, j - 2, slot).wait()

        for g in range(8):
            at = 8 * j + g
            yv[g] = dot(tf[at], x3[at])
            zv[g] = dot(tb[at], g3[at])
        tap = [[taps[i, l : l + 1, lanes] for l in range(3)] for i in range(3)]

        rn_j, wn_j = rn[j], wn[j]
        one = jnp.exp(rn_j)
        less = jnp.exp(-rn_j)

        def over(x):
            return jnp.sum(x, axis=0, keepdims=True)

        short = []
        for i in range(3):
            view = uf.at[j, i, length : length + 16, :]
            short.append(tap[i][0] * view[8:16, :] + tap[i][1] * view[7:15, :] + tap[i][2] * view[6:14, :])
        cot_next = jnp.where(last, 0.0, after[3, :, lanes].astype(F32)[0:8])
        x_next = (short[1] * short[2]).astype(BF16).astype(F32)[0:2]
        g_next = (cot_next * short[0]).astype(BF16).astype(F32)[0:1]
        h0 = over(wn_j)
        h1 = over(wn_j * less)
        long0 = over(wn_j * less * sout[j]) + h0 * x_next[0:1]
        long1 = over(wn_j * less * less * sout[j]) + h1 * x_next[0:1] + h0 * x_next[1:2]
        gg0 = over(wn_j * one * gin[j])
        gg1 = over(wn_j * one * one * gin[j]) - over(wn_j * one) * g_next
        row8 = row_iota(8)
        long_next = jnp.where(row8 == 0, long0, jnp.where(row8 == 1, long1, 0.0))
        gg_next = jnp.where(row8 == 0, gg0, jnp.where(row8 == 1, gg1, 0.0))
        ef[0, length : length + 8, :] = cot_next * long_next
        ef[1, length : length + 8, :] = gg_next * short[2]
        ef[2, length : length + 8, :] = gg_next * short[1]

        def finish(c, sums):
            s0 = pl.multiple_of(c * 16, 16)
            rows = pl.ds(s0, 16)
            longs = swap8([yv[g, rows, :] for g in range(8)])
            backs = swap8([zv[g, rows, :] for g in range(8)])
            sums = list(sums)
            for b in range(8):
                base = pl.multiple_of(b * BLK + s0, 16)
                short, windows = [], []
                for i in range(3):
                    view = uf.at[j, i, pl.ds(base, 24), :]
                    win = [view[8 - l : 24 - l, :] for l in range(3)]
                    windows.append(win)
                    short.append(tap[i][0] * win[0] + tap[i][1] * win[1] + tap[i][2] * win[2])
                stage[slot, 0, pl.ds(base, 16), :] = (short[0] * longs[b]).astype(BF16)
                grads = (
                    inb[3, j, pl.ds(base, 16), :].astype(F32) * longs[b],
                    backs[b] * short[2],
                    backs[b] * short[1],
                )
                for i in range(3):
                    ef[i, pl.ds(base, 16), :] = grads[i]
                    for l in range(3):
                        term = grads[i] * windows[i][l]
                        sums[3 * i + l] = sums[3 * i + l] + (term[0:8] + term[8:16])
            return tuple(sums)

        sums = lax.fori_loop(0, BLK // 16, finish, (jnp.zeros((8, LANES), F32),) * 9)
        for at in range(9):
            tsum[at : at + 1, lanes] = jnp.sum(sums[at], axis=0, keepdims=True)

        def spread(c, _):
            base = pl.multiple_of(c * 64, 64)
            for i in range(3):
                view = ef.at[i, pl.ds(base, 72), :]
                total = tap[i][0] * view[0:64, :] + tap[i][1] * view[1:65, :] + tap[i][2] * view[2:66, :]
                stage[slot, 1 + i, pl.ds(base, 64), :] = total.astype(BF16)
            return 0

        lax.fori_loop(0, length // 64, spread, 0)
        for i in range(4):
            put(i, j, slot).start()
        return 0

    for h in range(halves):
        for d in range(1, n):
            send(h, d).wait()
        lax.fori_loop(h * per, (h + 1) * per, combine, h)
        lax.fori_loop(h * per, (h + 1) * per, phase2, 0)

    tsum[9:16, :] = jnp.zeros((7, tsum.shape[1]), F32)
    trecv[me] = tsum[...].astype(BF16)
    grecv[me] = gacc[...]

    def give(d):
        peer = {"ctx": lax.rem(me + d, n)}
        return (
            pltpu.make_async_remote_copy(
                src_ref=trecv.at[me], dst_ref=trecv.at[me], send_sem=ts_sem.at[d], recv_sem=tr_sem.at[d],
                device_id=peer, device_id_type=MESH,
            ),
            pltpu.make_async_remote_copy(
                src_ref=grecv.at[me], dst_ref=grecv.at[me], send_sem=gs_sem.at[d], recv_sem=gr_sem.at[d],
                device_id=peer, device_id_type=MESH,
            ),
        )

    for d in range(1, n):
        for copy in give(d):
            copy.start()
    for j in range(max(0, tiles - 2), tiles):
        for i in range(4):
            put(i, j, j % 2).wait()
    for d in range(1, n):
        for copy in give(d):
            copy.wait()
    total = trecv[0].astype(F32)
    share = grecv[0]
    for s in range(1, n):
        total = total + trecv[s].astype(F32)
        share = share + grecv[s]
    taps_out[...] = total
    res_out[...] = share


def local(n, query, key, value, cot, taps, weights, rates):
    length, width = query.shape
    groups, modes = rates.shape
    tiles = width // LANES
    halves = 2 if tiles % 2 == 0 else 1
    per = tiles // halves
    big = jax.ShapeDtypeStruct((length, width), BF16)
    hbm = pl.BlockSpec(memory_space=pl.ANY)
    vmem = pl.BlockSpec(memory_space=pltpu.VMEM)
    dma = pltpu.SemaphoreType.DMA
    scratch = [
        pltpu.VMEM((4, tiles, length, LANES), BF16),
        pltpu.VMEM((tiles, 3, length + 16, LANES), F32),
        pltpu.VMEM((3, length + 8, LANES), F32),
        pltpu.VMEM((groups, 2 * BLK, LANES), BF16),
        pltpu.VMEM((groups, 2 * BLK, LANES), BF16),
        pltpu.VMEM((groups, BLK, 2 * LANES), BF16),
        pltpu.VMEM((groups, BLK, 2 * LANES), BF16),
        pltpu.VMEM((8, BLK, LANES), F32),
        pltpu.VMEM((8, BLK, LANES), F32),
        pltpu.VMEM((2, groups, modes, LANES), F32),
        pltpu.VMEM((groups, modes, LANES), F32),
        pltpu.VMEM((halves, 2, per, modes, LANES), F32),
        pltpu.VMEM((halves, n, per, modes, LANES), F32),
        pltpu.VMEM((3, 16, width), BF16),
        pltpu.VMEM((4, 16, width), BF16),
        pltpu.VMEM((tiles, modes, LANES), F32),
        pltpu.VMEM((tiles, modes, LANES), F32),
        pltpu.VMEM((groups, LANES), F32),
        pltpu.VMEM((groups, LANES), F32),
        pltpu.VMEM((tiles, modes, LANES), F32),
        pltpu.VMEM((tiles, modes, LANES), F32),
        pltpu.VMEM((2, 4, length, LANES), BF16),
        pltpu.VMEM((16, width), F32),
        pltpu.VMEM((n, 16, width), BF16),
        pltpu.VMEM((modes, LANES), F32),
        pltpu.VMEM((n, modes, LANES), F32),
        dma((4, tiles)), dma((7,)), dma((7,)), dma((halves, n)), dma((halves, n)), dma((2, 4)),
        dma((n,)), dma((n,)), dma((n,)), dma((n,)),
    ]
    mixed, grad_q, grad_k, grad_v, taps_sum, res_sum = pl.pallas_call(
        functools.partial(kernel, n, tiles, halves, length, modes),
        out_shape=(
            big, big, big, big,
            jax.ShapeDtypeStruct((16, width), F32),
            jax.ShapeDtypeStruct((modes, LANES), F32),
        ),
        in_specs=[hbm] * 4 + [vmem] * 3,
        out_specs=[hbm] * 4 + [vmem] * 2,
        scratch_shapes=scratch,
        compiler_params=pltpu.CompilerParams(
            collective_id=0, has_side_effects=True, vmem_limit_bytes=58 * 1024 * 1024
        ),
    )(query, key, value, cot, taps, rates, weights)
    grad_taps = taps_sum[:9].reshape(3, 3, width)
    return mixed, grad_q, grad_k, grad_v, grad_taps, res_sum[:, :groups].T


def solution(mesh):
    rows = P("ctx", "tp")
    n = mesh.shape["ctx"]
    return jax.shard_map(
        functools.partial(local, n),
        mesh=mesh,
        in_specs=(rows, rows, rows, rows, P(None, None, "tp"), P("tp", None), P("tp", None)),
        out_specs=(rows, rows, rows, rows, P(None, None, "tp"), P("tp", None)),
        check_vma=False,
    )
```

```python
import functools

import jax
import jax.numpy as jnp
from jax import lax
from jax.experimental import pallas as pl
from jax.experimental.pallas import tpu as pltpu
from jax.sharding import PartitionSpec as P

BLK = 128
LANES = 128
MEM = 16
HI = lax.Precision.HIGHEST
F32 = jnp.float32
BF16 = jnp.bfloat16
MESH = pl.DeviceIdType.MESH


def lane_iota(rows):
    return lax.broadcasted_iota(jnp.int32, (rows, LANES), 1)


def row_iota(rows):
    return lax.broadcasted_iota(jnp.int32, (rows, LANES), 0)


def turn(parts, piece):
    for d in (1, 2, 4):
        pick = (piece // d) % 2 == 1
        parts = [jnp.where(pick, parts[(g - d) % 8], parts[g]) for g in range(8)]
    return parts


def gather_groups(parts):
    piece = lane_iota(parts[0].shape[0]) // MEM
    parts = [pltpu.roll(p, MEM * b, 1) if b else p for b, p in enumerate(parts)]
    return turn([parts[-g % 8] for g in range(8)], piece)


def gather_blocks(parts):
    piece = lane_iota(parts[0].shape[0]) // MEM
    parts = turn([parts[-g % 8] for g in range(8)], piece)
    return [pltpu.roll(p, LANES - MEM * b, 1) if b else p for b, p in enumerate(parts)]


def split(value):
    high = value.astype(BF16)
    low = (value - high.astype(F32)).astype(BF16)
    return high, low


def dot(a, b, dims=((1,), (0,))):
    return lax.dot_general(a, b, (dims, ((), ())), preferred_element_type=F32)


def column(table, g):
    return jnp.broadcast_to(table[:, MEM * g : MEM * g + 1], table.shape)


def states_kernel(
    n, tiles, halves, length, modes,
    query, key, value, cot, taps, rates, weights,
    xs_out, gs_out, tf_out, tb_out, sf, sb, halo_out, after_out, rn, wn, sout, gin, gacc,
    inb, uf, xs, gs, tf, tb, fs, gb, st, rs, halo, after, r3, w3,
    in_sem, hs_sem, hr_sem, ss_sem, sr_sem, table_sem, part_sem,
):
    me = lax.axis_index("ctx")
    per = tiles // halves
    barrier = pltpu.get_barrier_semaphore()
    for d in range(1, n):
        pl.semaphore_signal(barrier, inc=1, device_id={"ctx": lax.rem(me + d, n)}, device_id_type=MESH)

    streams = (query, key, value, cot)

    def fetch(i, j):
        return pltpu.make_async_copy(
            streams[i].at[:, pl.ds(pl.multiple_of(j * LANES, LANES), LANES)], inb.at[i, j], in_sem.at[i, j]
        )

    for j in range(tiles):
        for i in range(4):
            fetch(i, j).start()

    def exact(a, b, dims):
        return lax.dot_general(a, b, (dims, ((), ())), precision=HI, preferred_element_type=F32)

    repeat = (lane_iota(modes) % modes == row_iota(modes)).astype(F32)
    for j in range(tiles):
        group = (lane_iota(8 * tiles) // MEM + 8 * j == row_iota(8 * tiles)).astype(F32)
        rn[j] = exact(rates[...], group, ((1,), (0,)))
        wn[j] = exact(weights[...], group, ((1,), (0,)))
    r3[...] = exact(rates[...], repeat, ((0,), (0,)))
    w3[...] = exact(weights[...], repeat, ((0,), (0,)))

    pl.semaphore_wait(barrier, n - 1)

    def behind(i):
        return pltpu.make_async_remote_copy(
            src_ref=streams[i].at[pl.ds(length - 16, 16), :], dst_ref=halo.at[i],
            send_sem=hs_sem.at[i], recv_sem=hr_sem.at[i],
            device_id={"ctx": lax.rem(me + 1, n)}, device_id_type=MESH,
        )

    def ahead(i):
        return pltpu.make_async_remote_copy(
            src_ref=streams[i].at[pl.ds(0, 16), :], dst_ref=after.at[i],
            send_sem=hs_sem.at[3 + i], recv_sem=hr_sem.at[3 + i],
            device_id={"ctx": lax.rem(me + n - 1, n)}, device_id_type=MESH,
        )

    for i in range(3):
        behind(i).start()
    for i in range(4):
        ahead(i).start()

    t_row = row_iota(BLK).astype(F32)
    lane_f = lane_iota(modes).astype(F32)
    lane_b = lane_iota(BLK)
    causal = row_iota(BLK) >= lane_iota(BLK)
    anti = row_iota(BLK) <= lane_iota(BLK)

    def build(j, _):
        rn_j = rn[j]
        for g in range(8):
            at = 8 * j + g
            r_row = r3[pl.ds(at, 1), :]
            w_row = w3[pl.ds(at, 1), :]
            r_col = column(rn_j, g)
            pad = jnp.zeros((LANES - 3 * modes, LANES), BF16)
            for ref, reach, peer, mask in (
                (tf, t_row + 1.0, lane_f + 1.0, causal),
                (tb, (BLK - 1.0) - t_row, (BLK - 1.0) - lane_f, anti),
            ):
                high, low = split(w_row * jnp.exp(-r_row * reach))
                zero = jnp.zeros_like(high)
                left = jnp.where(lane_b < 2 * modes, high, jnp.where(lane_b < 3 * modes, low, zero))
                v_high, v_low = split(jnp.exp(r_col * peer))
                right = jnp.concatenate([v_high, v_low, v_high, pad], axis=0)
                table = dot(left, right)
                ref[at, :, 0:BLK] = jnp.where(mask, table, 0.0).astype(BF16)
                ref[at, :, BLK : 2 * BLK] = left
        return 0

    lax.fori_loop(0, tiles, build, 0)
    tables = [
        pltpu.make_async_copy(source, target, table_sem.at[at])
        for at, (source, target) in enumerate(((tf, tf_out), (tb, tb_out)))
    ]
    for copy in tables:
        copy.start()

    for i in range(3):
        behind(i).wait()
    for i in range(4):
        ahead(i).wait()
    halo_out[...] = halo[...]
    after_out[...] = after[...]

    first = (me == 0)
    lane16 = lane_iota(modes)
    piece16 = lane16 // MEM

    def parts(j):
        rows = pl.ds(8 * j, 8)
        return [
            pltpu.make_async_copy(source.at[rows], target.at[rows], part_sem.at[at, j])
            for at, (source, target) in enumerate(((xs, xs_out), (gs, gs_out)))
        ]

    def phase1(j, _):
        lanes = pl.ds(pl.multiple_of(j * LANES, LANES), LANES)
        for i in range(4):
            fetch(i, j).wait()
        for i in range(3):
            prior = halo[i, :, lanes].astype(F32)[8:16]
            uf[i, 0:8, :] = jnp.where(first, 0.0, prior)

        def widen(c, _):
            for i in range(3):
                rows = pl.ds(pl.multiple_of(c * 64, 64), 64)
                uf[i, pl.ds(pl.multiple_of(c * 64 + 8, 8), 64), :] = inb[i, j, rows, :].astype(F32)
            return 0

        lax.fori_loop(0, length // 64, widen, 0)
        tap = [[taps[i, l : l + 1, lanes] for l in range(3)] for i in range(3)]

        def gate(c, _):
            s0 = pl.multiple_of(c * 16, 16)
            forward, backward = [], []
            for b in range(8):
                base = pl.multiple_of(b * BLK + s0, 16)
                short = []
                for i in range(3):
                    view = uf.at[i, pl.ds(base, 24), :]
                    total = tap[i][0] * view[8:24, :] + tap[i][1] * view[7:23, :] + tap[i][2] * view[6:22, :]
                    short.append(total)
                forward.append(short[1] * short[2])
                backward.append(inb[3, j, pl.ds(base, 16), :].astype(F32) * short[0])
            for ref, parts in ((xs, forward), (gs, backward)):
                for g, part in enumerate(gather_groups(parts)):
                    ref[8 * j + g, pl.ds(s0, 16), :] = part.astype(BF16)
            return 0

        lax.fori_loop(0, BLK // 16, gate, 0)

        rn_j = rn[j]
        ahead_state = jnp.zeros((modes, LANES), F32)
        back_state = jnp.zeros((modes, LANES), F32)
        for g in range(8):
            at = 8 * j + g
            r_col = column(rn_j, g)
            absorb = jnp.concatenate(split(jnp.exp(-r_col * ((BLK - 1.0) - lane_f))), axis=0)
            ends2 = dot(absorb, xs[at])
            ends = ends2[0:modes] + ends2[modes : 2 * modes]
            emit = jnp.concatenate(split(jnp.exp(-r_col * (lane_f + 1.0))), axis=0)
            starts2 = dot(emit, gs[at])
            starts = starts2[0:modes] + starts2[modes : 2 * modes]
            gb[at] = starts
            power = jnp.exp(-r_col * float(BLK))
            block = (piece16 + 8 - g) % 8
            for d in (1, 2, 4):
                moved = pltpu.roll(ends, MEM * d, 1)
                ends = ends + jnp.where(block >= d, power * moved, 0.0)
                moved = pltpu.roll(starts, LANES - MEM * d, 1)
                starts = starts + jnp.where(block < 8 - d, power * moved, 0.0)
                power = power * power
            ends_next = pltpu.roll(ends, MEM, 1)
            starts_prev = pltpu.roll(starts, LANES - MEM, 1)
            fs[0, at] = jnp.where(block == 0, 0.0, ends_next)
            fs[1, at] = jnp.where(block == 7, 0.0, starts_prev)
            ahead_state = jnp.where(piece16 == g, ends_next, ahead_state)
            back_state = jnp.where(piece16 == g, starts, back_state)
        st[j // per, 0, j % per] = ahead_state
        st[j // per, 1, j % per] = back_state
        for copy in parts(j):
            copy.start()
        return 0

    def send(h, d):
        return pltpu.make_async_remote_copy(
            src_ref=st.at[h, (me + d) // n], dst_ref=rs.at[h, d],
            send_sem=ss_sem.at[h, d], recv_sem=sr_sem.at[h, d],
            device_id={"ctx": lax.rem(me + d, n)}, device_id_type=MESH,
        )

    for h in range(halves):
        lax.fori_loop(h * per, (h + 1) * per, phase1, 0)
        for d in range(1, n):
            send(h, d).start()

    gacc[...] = jnp.zeros_like(gacc)

    def within(j, _):
        rn_j = rn[j]
        total = gacc[...]
        for g in range(8):
            at = 8 * j + g
            r_col = column(rn_j, g)
            pairs = dot(xs[at], gs[at].astype(F32).T.astype(BF16))
            pairs = jnp.where(anti, pairs, 0.0).astype(BF16)
            rise = jnp.concatenate(split(jnp.exp(r_col * lane_f)), axis=0)
            both = dot(rise, pairs)
            terms = (both[0:modes] + both[modes : 2 * modes]) * jnp.exp(-r_col * lane_f)
            total = jnp.where(lane16 == at, total + jnp.sum(terms, axis=1, keepdims=True), total)
        gacc[...] = total
        return 0

    lax.fori_loop(0, tiles, within, 0)

    def combine(j, h):
        jj = j - h * per
        rn_j = rn[j]
        whole = jnp.exp(-rn_j * float(length))
        into = jnp.zeros((modes, LANES), F32)
        back = jnp.zeros((modes, LANES), F32)
        for e in range(n - 1, 0, -1):
            into = whole * into + jnp.where(e <= me, rs[h, e, jj], 0.0)
            back = whole * back + jnp.where(e <= n - 1 - me, rs[h, n - e, jj], 0.0)
        sout[j] = whole * into + st[h, 0, jj]
        gin[j] = back
        total = gacc[...]
        for g in range(8):
            at = 8 * j + g
            r_col = column(rn_j, g)
            here = []
            for state in (into, back):
                spread = jnp.where(piece16 == g, state, 0.0)
                for d in (1, 2, 4):
                    spread = spread + pltpu.roll(spread, MEM * d, 1)
                here.append(spread)
            step = ((piece16 + 8 - g) % 8).astype(F32) * float(BLK)
            before = fs[0, at] + jnp.exp(-r_col * step) * here[0]
            behind_ = fs[1, at] + jnp.exp(-r_col * ((7.0 * BLK) - step)) * here[1]
            total = jnp.where(lane16 == at, total + jnp.sum(gb[at] * before, axis=1, keepdims=True), total)
            for ref, state in ((sf, before), (sb, behind_)):
                high, low = split(state)
                ref[at] = jnp.concatenate([high, low, high], axis=0)
        gacc[...] = total
        return h

    for h in range(halves):
        for d in range(1, n):
            send(h, d).wait()
        lax.fori_loop(h * per, (h + 1) * per, combine, h)
    for copy in tables:
        copy.wait()
    for j in range(tiles):
        for copy in parts(j):
            copy.wait()


def outputs_kernel(
    n, length, modes,
    query, key, value, cot, taps, xs, gs, tf, tb, sf, sb, halo, after, rn, wn, sout, gin,
    mixed, grad_q, grad_k, grad_v, tsum,
    uf, ef, yv, zv,
):
    first = lax.axis_index("ctx") == 0
    last = lax.axis_index("ctx") == n - 1
    for i in range(3):
        uf[i, 0:8, :] = jnp.where(first, 0.0, halo[i].astype(F32)[8:16])
        uf[i, 8 + length : 16 + length, :] = jnp.where(last, 0.0, after[i].astype(F32)[0:8])
    streams = (query, key, value)

    def widen(c, _):
        for i in range(3):
            rows = pl.ds(pl.multiple_of(c * 64, 64), 64)
            uf[i, pl.ds(pl.multiple_of(c * 64 + 8, 8), 64), :] = streams[i][rows, :].astype(F32)
        return 0

    lax.fori_loop(0, length // 64, widen, 0)
    zeros = jnp.zeros((BLK - 3 * modes, LANES), BF16)
    for g in range(8):
        yv[g] = dot(tf[g], jnp.concatenate([xs[g], sf[g], zeros], axis=0))
        zv[g] = dot(tb[g], jnp.concatenate([gs[g], sb[g], zeros], axis=0))
    tap = [[taps[i, l : l + 1, :] for l in range(3)] for i in range(3)]

    rn_j, wn_j = rn[0], wn[0]
    one = jnp.exp(rn_j)
    less = jnp.exp(-rn_j)

    def over(x):
        return jnp.sum(x, axis=0, keepdims=True)

    short = []
    for i in range(3):
        view = uf.at[i, length : length + 16, :]
        short.append(tap[i][0] * view[8:16, :] + tap[i][1] * view[7:15, :] + tap[i][2] * view[6:14, :])
    cot_next = jnp.where(last, 0.0, after[3].astype(F32)[0:8])
    x_next = (short[1] * short[2]).astype(BF16).astype(F32)[0:2]
    g_next = (cot_next * short[0]).astype(BF16).astype(F32)[0:1]
    h0 = over(wn_j)
    h1 = over(wn_j * less)
    long0 = over(wn_j * less * sout[0]) + h0 * x_next[0:1]
    long1 = over(wn_j * less * less * sout[0]) + h1 * x_next[0:1] + h0 * x_next[1:2]
    gg0 = over(wn_j * one * gin[0])
    gg1 = over(wn_j * one * one * gin[0]) - over(wn_j * one) * g_next
    row8 = row_iota(8)
    long_next = jnp.where(row8 == 0, long0, jnp.where(row8 == 1, long1, 0.0))
    gg_next = jnp.where(row8 == 0, gg0, jnp.where(row8 == 1, gg1, 0.0))
    ef[0, length : length + 8, :] = cot_next * long_next
    ef[1, length : length + 8, :] = gg_next * short[2]
    ef[2, length : length + 8, :] = gg_next * short[1]

    def finish(c, sums):
        s0 = pl.multiple_of(c * 16, 16)
        rows = pl.ds(s0, 16)
        longs = gather_blocks([yv[g, rows, :] for g in range(8)])
        backs = gather_blocks([zv[g, rows, :] for g in range(8)])
        sums = list(sums)
        for b in range(8):
            base = pl.multiple_of(b * BLK + s0, 16)
            short, windows = [], []
            for i in range(3):
                view = uf.at[i, pl.ds(base, 24), :]
                win = [view[8 - l : 24 - l, :] for l in range(3)]
                windows.append(win)
                short.append(tap[i][0] * win[0] + tap[i][1] * win[1] + tap[i][2] * win[2])
            mixed[pl.ds(base, 16), :] = (short[0] * longs[b]).astype(BF16)
            grads = (
                cot[pl.ds(base, 16), :].astype(F32) * longs[b],
                backs[b] * short[2],
                backs[b] * short[1],
            )
            for i in range(3):
                ef[i, pl.ds(base, 16), :] = grads[i]
                for l in range(3):
                    term = grads[i] * windows[i][l]
                    sums[3 * i + l] = sums[3 * i + l] + (term[0:8] + term[8:16])
        return tuple(sums)

    sums = lax.fori_loop(0, BLK // 16, finish, (jnp.zeros((8, LANES), F32),) * 9)
    for at in range(9):
        tsum[at : at + 1, :] = jnp.sum(sums[at], axis=0, keepdims=True)
    tsum[9:16, :] = jnp.zeros((7, LANES), F32)

    def spread(c, _):
        base = pl.multiple_of(c * 64, 64)
        for i in range(3):
            view = ef.at[i, pl.ds(base, 72), :]
            total = tap[i][0] * view[0:64, :] + tap[i][1] * view[1:65, :] + tap[i][2] * view[2:66, :]
            (grad_q, grad_k, grad_v)[i][pl.ds(base, 64), :] = total.astype(BF16)
        return 0

    lax.fori_loop(0, length // 64, spread, 0)


def sums_kernel(n, tiles, modes, tsum, gacc, taps_out, res_out, box, send_sem, recv_sem):
    me = lax.axis_index("ctx")
    barrier = pltpu.get_barrier_semaphore()
    for d in range(1, n):
        pl.semaphore_signal(barrier, inc=1, device_id={"ctx": lax.rem(me + d, n)}, device_id_type=MESH)
    for j in range(tiles):
        box[me, 16 * j : 16 * (j + 1), :] = tsum[:, LANES * j : LANES * (j + 1)].astype(BF16)
    high, low = split(gacc[...])
    box[me, 16 * tiles : 16 * tiles + modes, :] = high
    box[me, 16 * tiles + modes : 16 * tiles + 2 * modes, :] = low
    pl.semaphore_wait(barrier, n - 1)

    def give(d):
        return pltpu.make_async_remote_copy(
            src_ref=box.at[me], dst_ref=box.at[me], send_sem=send_sem.at[d], recv_sem=recv_sem.at[d],
            device_id={"ctx": lax.rem(me + d, n)}, device_id_type=MESH,
        )

    for d in range(1, n):
        give(d).start()
    for d in range(1, n):
        give(d).wait()
    total = box[0].astype(F32)
    for s in range(1, n):
        total = total + box[s].astype(F32)
    for j in range(tiles):
        taps_out[:, LANES * j : LANES * (j + 1)] = total[16 * j : 16 * (j + 1)]
    res_out[...] = total[16 * tiles : 16 * tiles + modes] + total[16 * tiles + modes :]


def local(n, query, key, value, cot, taps, weights, rates):
    length, width = query.shape
    groups, modes = rates.shape
    tiles = width // LANES
    halves = 2 if tiles % 2 == 0 else 1
    per = tiles // halves
    hbm = pl.BlockSpec(memory_space=pl.ANY)
    vmem = pl.BlockSpec(memory_space=pltpu.VMEM)
    dma = pltpu.SemaphoreType.DMA
    shape = jax.ShapeDtypeStruct
    natural = shape((tiles, modes, LANES), F32)
    part = shape((groups, BLK, LANES), BF16)
    table = shape((groups, BLK, 2 * LANES), BF16)
    carry = shape((groups, 3 * modes, LANES), BF16)
    *middle, gacc = pl.pallas_call(
        functools.partial(states_kernel, n, tiles, halves, length, modes),
        out_shape=(
            part, part, table, table, carry, carry,
            shape((3, 16, width), BF16), shape((4, 16, width), BF16),
            natural, natural, natural, natural, shape((modes, LANES), F32),
        ),
        in_specs=[hbm] * 4 + [vmem] * 3,
        out_specs=[hbm] * 4 + [vmem] * 9,
        scratch_shapes=[
            pltpu.VMEM((4, tiles, length, LANES), BF16),
            pltpu.VMEM((3, length + 16, LANES), F32),
            pltpu.VMEM((groups, BLK, LANES), BF16),
            pltpu.VMEM((groups, BLK, LANES), BF16),
            pltpu.VMEM((groups, BLK, 2 * LANES), BF16),
            pltpu.VMEM((groups, BLK, 2 * LANES), BF16),
            pltpu.VMEM((2, groups, modes, LANES), F32),
            pltpu.VMEM((groups, modes, LANES), F32),
            pltpu.VMEM((halves, 2, per, modes, LANES), F32),
            pltpu.VMEM((halves, n, per, modes, LANES), F32),
            pltpu.VMEM((3, 16, width), BF16),
            pltpu.VMEM((4, 16, width), BF16),
            pltpu.VMEM((groups, LANES), F32),
            pltpu.VMEM((groups, LANES), F32),
            dma((4, tiles)), dma((7,)), dma((7,)), dma((halves, n)), dma((halves, n)), dma((2,)), dma((2, tiles)),
        ],
        compiler_params=pltpu.CompilerParams(
            collective_id=0, has_side_effects=True, vmem_limit_bytes=60 * 1024 * 1024
        ),
    )(query, key, value, cot, taps, rates.T, weights.T)

    def stack(*shape):
        return pl.BlockSpec(shape, lambda j: (j, 0, 0))

    def wide(*shape):
        return pl.BlockSpec(shape, lambda j: (0, 0, j))

    tokens = pl.BlockSpec((length, LANES), lambda j: (0, j))
    big = shape((length, width), BF16)
    state = stack(1, modes, LANES)
    mixed, grad_q, grad_k, grad_v, tsum = pl.pallas_call(
        functools.partial(outputs_kernel, n, length, modes),
        grid=(tiles,),
        out_shape=(big, big, big, big, shape((16, width), F32)),
        in_specs=[
            tokens, tokens, tokens, tokens, wide(3, 3, LANES),
            stack(8, BLK, LANES), stack(8, BLK, LANES), stack(8, BLK, 2 * LANES), stack(8, BLK, 2 * LANES),
            stack(8, 3 * modes, LANES), stack(8, 3 * modes, LANES),
            wide(3, 16, LANES), wide(4, 16, LANES), state, state, state, state,
        ],
        out_specs=[tokens] * 4 + [pl.BlockSpec((16, LANES), lambda j: (0, j))],
        scratch_shapes=[
            pltpu.VMEM((3, length + 16, LANES), F32),
            pltpu.VMEM((3, length + 8, LANES), F32),
            pltpu.VMEM((8, BLK, LANES), F32),
            pltpu.VMEM((8, BLK, LANES), F32),
        ],
        compiler_params=pltpu.CompilerParams(
            dimension_semantics=("arbitrary",), vmem_limit_bytes=60 * 1024 * 1024
        ),
    )(query, key, value, cot, taps, *middle)
    rows = 16 * tiles + 2 * modes
    taps_sum, res_sum = pl.pallas_call(
        functools.partial(sums_kernel, n, tiles, modes),
        out_shape=(shape((16, width), F32), shape((modes, LANES), F32)),
        in_specs=[vmem] * 2,
        out_specs=[vmem] * 2,
        scratch_shapes=[pltpu.VMEM((n, rows, LANES), BF16), dma((n,)), dma((n,))],
        compiler_params=pltpu.CompilerParams(
            collective_id=1, has_side_effects=True, vmem_limit_bytes=60 * 1024 * 1024
        ),
    )(tsum, gacc)
    grad_taps = taps_sum[:9].reshape(3, 3, width)
    return mixed, grad_q, grad_k, grad_v, grad_taps, res_sum[:, :groups].T


def solution(mesh):
    rows = P("ctx", "tp")
    n = mesh.shape["ctx"]
    return jax.shard_map(
        functools.partial(local, n),
        mesh=mesh,
        in_specs=(rows, rows, rows, rows, P(None, None, "tp"), P("tp", None), P("tp", None)),
        out_specs=(rows, rows, rows, rows, P(None, None, "tp"), P("tp", None)),
        check_vma=False,
    )
```

```python
import functools

import jax
import jax.numpy as jnp
from jax import lax
from jax.experimental import pallas as pl
from jax.experimental.pallas import tpu as pltpu
from jax.sharding import PartitionSpec as P

BLK = 128
LANES = 128
MEM = 16
HI = lax.Precision.HIGHEST
F32 = jnp.float32
BF16 = jnp.bfloat16
MESH = pl.DeviceIdType.MESH


def lane_iota(rows):
    return lax.broadcasted_iota(jnp.int32, (rows, LANES), 1)


def row_iota(rows):
    return lax.broadcasted_iota(jnp.int32, (rows, LANES), 0)


def turn(parts, piece):
    for d in (1, 2, 4):
        pick = (piece // d) % 2 == 1
        parts = [jnp.where(pick, parts[(g - d) % 8], parts[g]) for g in range(8)]
    return parts


def gather_groups(parts):
    piece = lane_iota(parts[0].shape[0]) // MEM
    parts = [pltpu.roll(p, MEM * b, 1) if b else p for b, p in enumerate(parts)]
    return turn([parts[-g % 8] for g in range(8)], piece)


def gather_blocks(parts):
    piece = lane_iota(parts[0].shape[0]) // MEM
    parts = turn([parts[-g % 8] for g in range(8)], piece)
    return [pltpu.roll(p, LANES - MEM * b, 1) if b else p for b, p in enumerate(parts)]


def split(value):
    high = value.astype(BF16)
    low = (value - high.astype(F32)).astype(BF16)
    return high, low


def dot(a, b, dims=((1,), (0,))):
    return lax.dot_general(a, b, (dims, ((), ())), preferred_element_type=F32)


def column(table, g):
    return jnp.broadcast_to(table[:, MEM * g : MEM * g + 1], table.shape)


def filters_kernel(
    n, tiles, halves, length, modes,
    query, key, value, cot, taps, rates, weights,
    long_out, back_out, halo_out, after_out, rn, wn, sout, gin, taps_out, res_out,
    inb, uf, xs, gs, tf, tb, sf, sb, fs, gb, st, rs, halo, after, r3, w3, gacc, yv, zv, stage, tsum, *rest,
):
    early, late = rest[0:2]
    in_sem, hs_sem, hr_sem, ss_sem, sr_sem, out_sem, ts_sem, tr_sem = rest[2:]
    me = lax.axis_index("ctx")
    per = tiles // halves
    barrier = pltpu.get_barrier_semaphore()
    for d in range(1, n):
        pl.semaphore_signal(barrier, inc=1, device_id={"ctx": lax.rem(me + d, n)}, device_id_type=MESH)

    streams = (query, key, value, cot)

    def fetch(i, j):
        return pltpu.make_async_copy(
            streams[i].at[:, pl.ds(pl.multiple_of(j * LANES, LANES), LANES)], inb.at[i, j], in_sem.at[i, j]
        )

    for j in range(tiles):
        for i in range(4):
            fetch(i, j).start()

    def exact(a, b, dims):
        return lax.dot_general(a, b, (dims, ((), ())), precision=HI, preferred_element_type=F32)

    repeat = (lane_iota(modes) % modes == row_iota(modes)).astype(F32)
    for j in range(tiles):
        group = (lane_iota(8 * tiles) // MEM + 8 * j == row_iota(8 * tiles)).astype(F32)
        rn[j] = exact(rates[...], group, ((1,), (0,)))
        wn[j] = exact(weights[...], group, ((1,), (0,)))
    r3[...] = exact(rates[...], repeat, ((0,), (0,)))
    w3[...] = exact(weights[...], repeat, ((0,), (0,)))

    t_row = row_iota(BLK).astype(F32)
    lane_f = lane_iota(modes).astype(F32)
    lane_b = lane_iota(BLK)
    causal = row_iota(BLK) >= lane_iota(BLK)
    anti = row_iota(BLK) <= lane_iota(BLK)

    def build(j, _):
        rn_j = rn[j]
        for g in range(8):
            at = 8 * j + g
            r_row = r3[pl.ds(at, 1), :]
            w_row = w3[pl.ds(at, 1), :]
            r_col = column(rn_j, g)
            pad = jnp.zeros((LANES - 3 * modes, LANES), BF16)
            for ref, reach, peer, mask in (
                (tf, t_row + 1.0, lane_f + 1.0, causal),
                (tb, (BLK - 1.0) - t_row, (BLK - 1.0) - lane_f, anti),
            ):
                high, low = split(w_row * jnp.exp(-r_row * reach))
                zero = jnp.zeros_like(high)
                left = jnp.where(lane_b < 2 * modes, high, jnp.where(lane_b < 3 * modes, low, zero))
                v_high, v_low = split(jnp.exp(r_col * peer))
                right = jnp.concatenate([v_high, v_low, v_high, pad], axis=0)
                table = dot(left, right)
                ref[at, :, 0:BLK] = jnp.where(mask, table, 0.0).astype(BF16)
                ref[at, :, BLK : 2 * BLK] = left
        return 0

    lax.fori_loop(0, tiles // 2, build, 0)
    pl.semaphore_wait(barrier, n - 1)

    def behind(i):
        return pltpu.make_async_remote_copy(
            src_ref=streams[i].at[pl.ds(length - 16, 16), :], dst_ref=halo.at[i],
            send_sem=hs_sem.at[i], recv_sem=hr_sem.at[i],
            device_id={"ctx": lax.rem(me + 1, n)}, device_id_type=MESH,
        )

    def ahead(i):
        return pltpu.make_async_remote_copy(
            src_ref=streams[i].at[pl.ds(0, 16), :], dst_ref=after.at[i],
            send_sem=hs_sem.at[3 + i], recv_sem=hr_sem.at[3 + i],
            device_id={"ctx": lax.rem(me + n - 1, n)}, device_id_type=MESH,
        )

    for i in range(3):
        behind(i).start()
    for i in range(4):
        ahead(i).start()

    lax.fori_loop(tiles // 2, tiles, build, 0)

    for i in range(3):
        behind(i).wait()
    for i in range(4):
        ahead(i).wait()
    halo_out[...] = halo[...]
    after_out[...] = after[...]

    first = (me == 0)
    lane16 = lane_iota(modes)
    piece16 = lane16 // MEM

    def phase1(j, _):
        lanes = pl.ds(pl.multiple_of(j * LANES, LANES), LANES)
        for i in range(4):
            fetch(i, j).wait()
        for i in range(3):
            prior = halo[i, :, lanes].astype(F32)[8:16]
            uf[j, i, 0:8, :] = jnp.where(first, 0.0, prior)

        def widen(c, _):
            for i in range(3):
                rows = pl.ds(pl.multiple_of(c * 64, 64), 64)
                uf[j, i, pl.ds(pl.multiple_of(c * 64 + 8, 8), 64), :] = inb[i, j, rows, :].astype(F32)
            return 0

        lax.fori_loop(0, length // 64, widen, 0)
        tap = [[taps[i, l : l + 1, lanes] for l in range(3)] for i in range(3)]

        def gate(c, _):
            s0 = pl.multiple_of(c * 16, 16)
            forward, backward = [], []
            for b in range(8):
                base = pl.multiple_of(b * BLK + s0, 16)
                short = []
                for i in range(3):
                    view = uf.at[j, i, pl.ds(base, 24), :]
                    total = tap[i][0] * view[8:24, :] + tap[i][1] * view[7:23, :] + tap[i][2] * view[6:22, :]
                    short.append(total)
                forward.append(short[1] * short[2])
                backward.append(inb[3, j, pl.ds(base, 16), :].astype(F32) * short[0])
            for ref, parts in ((xs, forward), (gs, backward)):
                for g, part in enumerate(gather_groups(parts)):
                    ref[8 * j + g, pl.ds(s0, 16), :] = part.astype(BF16)
            return 0

        lax.fori_loop(0, BLK // 16, gate, 0)

        rn_j = rn[j]
        ahead_state = jnp.zeros((modes, LANES), F32)
        back_state = jnp.zeros((modes, LANES), F32)
        for g in range(8):
            at = 8 * j + g
            r_col = column(rn_j, g)
            absorb = jnp.concatenate(split(jnp.exp(-r_col * ((BLK - 1.0) - lane_f))), axis=0)
            ends2 = dot(absorb, xs[at])
            ends = ends2[0:modes] + ends2[modes : 2 * modes]
            emit = jnp.concatenate(split(jnp.exp(-r_col * (lane_f + 1.0))), axis=0)
            starts2 = dot(emit, gs[at])
            starts = starts2[0:modes] + starts2[modes : 2 * modes]
            gb[at] = starts
            power = jnp.exp(-r_col * float(BLK))
            block = (piece16 + 8 - g) % 8
            for d in (1, 2, 4):
                moved = pltpu.roll(ends, MEM * d, 1)
                ends = ends + jnp.where(block >= d, power * moved, 0.0)
                moved = pltpu.roll(starts, LANES - MEM * d, 1)
                starts = starts + jnp.where(block < 8 - d, power * moved, 0.0)
                power = power * power
            ends_next = pltpu.roll(ends, MEM, 1)
            starts_prev = pltpu.roll(starts, LANES - MEM, 1)
            fs[0, at] = jnp.where(block == 0, 0.0, ends_next)
            fs[1, at] = jnp.where(block == 7, 0.0, starts_prev)
            ahead_state = jnp.where(piece16 == g, ends_next, ahead_state)
            back_state = jnp.where(piece16 == g, starts, back_state)
        st[j // per, 0, j % per] = ahead_state.astype(BF16)
        st[j // per, 1, j % per] = back_state.astype(BF16)
        return 0

    def send(h, d):
        return pltpu.make_async_remote_copy(
            src_ref=st.at[h, (me + d) // n], dst_ref=rs.at[h, d],
            send_sem=ss_sem.at[h, d], recv_sem=sr_sem.at[h, d],
            device_id={"ctx": lax.rem(me + d, n)}, device_id_type=MESH,
        )

    for h in range(halves):
        lax.fori_loop(h * per, (h + 1) * per, phase1, 0)
        for d in range(1, n):
            send(h, d).start()

    gacc[...] = jnp.zeros_like(gacc)

    def within(j, _):
        rn_j = rn[j]
        total = gacc[...]
        for g in range(8):
            at = 8 * j + g
            r_col = column(rn_j, g)
            pairs = dot(xs[at], gs[at].astype(F32).T.astype(BF16))
            pairs = jnp.where(anti, pairs, 0.0).astype(BF16)
            rise = jnp.concatenate(split(jnp.exp(r_col * lane_f)), axis=0)
            both = dot(rise, pairs)
            terms = (both[0:modes] + both[modes : 2 * modes]) * jnp.exp(-r_col * lane_f)
            total = jnp.where(lane16 == at, total + jnp.sum(terms, axis=1, keepdims=True), total)
        gacc[...] = total
        return 0

    lax.fori_loop(0, tiles, within, 0)

    def combine(j, h):
        jj = j - h * per
        rn_j = rn[j]
        whole = jnp.exp(-rn_j * float(length))
        into = jnp.zeros((modes, LANES), F32)
        back = jnp.zeros((modes, LANES), F32)
        for e in range(n - 1, 0, -1):
            into = whole * into + jnp.where(e <= me, rs[h, e, jj].astype(F32), 0.0)
            back = whole * back + jnp.where(e <= n - 1 - me, rs[h, n - e, jj].astype(F32), 0.0)
        sout[j] = whole * into + st[h, 0, jj].astype(F32)
        gin[j] = back
        total = gacc[...]
        for g in range(8):
            at = 8 * j + g
            r_col = column(rn_j, g)
            here = []
            for state in (into, back):
                spread = jnp.where(piece16 == g, state, 0.0)
                for d in (1, 2, 4):
                    spread = spread + pltpu.roll(spread, MEM * d, 1)
                here.append(spread)
            step = ((piece16 + 8 - g) % 8).astype(F32) * float(BLK)
            before = fs[0, at] + jnp.exp(-r_col * step) * here[0]
            behind_ = fs[1, at] + jnp.exp(-r_col * ((7.0 * BLK) - step)) * here[1]
            total = jnp.where(lane16 == at, total + jnp.sum(gb[at] * before, axis=1, keepdims=True), total)
            for ref, state in ((sf, before), (sb, behind_)):
                high, low = split(state)
                ref[at] = jnp.concatenate([high, low, high], axis=0)
        gacc[...] = total
        return h

    for h in range(halves):
        for d in range(1, n):
            send(h, d).wait()
        lax.fori_loop(h * per, (h + 1) * per, combine, h)

    def put(i, j, slot):
        return pltpu.make_async_copy(stage.at[slot, i], (long_out, back_out)[i].at[j], out_sem.at[slot, i])

    pad = jnp.zeros((BLK - 3 * modes, LANES), BF16)

    def phase2(j, _):
        lanes = pl.ds(pl.multiple_of(j * LANES, LANES), LANES)
        slot = j % 2

        @pl.when(j >= 2)
        def _():
            for i in range(2):
                put(i, j - 2, slot).wait()

        for g in range(8):
            at = 8 * j + g
            yv[g] = dot(tf[at], jnp.concatenate([xs[at], sf[at], pad], axis=0))
            zv[g] = dot(tb[at], jnp.concatenate([gs[at], sb[at], pad], axis=0))
        tap = [[taps[i, l : l + 1, lanes] for l in range(3)] for i in range(3)]

        def finish(c, sums):
            s0 = pl.multiple_of(c * 16, 16)
            rows = pl.ds(s0, 16)
            longs = gather_blocks([yv[g, rows, :] for g in range(8)])
            backs = gather_blocks([zv[g, rows, :] for g in range(8)])
            sums = list(sums)
            for b in range(8):
                base = pl.multiple_of(b * BLK + s0, 16)
                stage[slot, 0, pl.ds(base, 16), :] = longs[b].astype(BF16)
                stage[slot, 1, pl.ds(base, 16), :] = backs[b].astype(BF16)
                short, windows = [], []
                for i in range(3):
                    view = uf.at[j, i, pl.ds(base, 24), :]
                    win = [view[8 - l : 24 - l, :] for l in range(3)]
                    windows.append(win)
                    if i:
                        short.append(tap[i][0] * win[0] + tap[i][1] * win[1] + tap[i][2] * win[2])
                grads = (
                    inb[3, j, pl.ds(base, 16), :].astype(F32) * longs[b],
                    backs[b] * short[1],
                    backs[b] * short[0],
                )
                for i in range(3):
                    for l in range(3):
                        term = grads[i] * windows[i][l]
                        sums[3 * i + l] = sums[3 * i + l] + (term[0:8] + term[8:16])
            return tuple(sums)

        sums = lax.fori_loop(0, BLK // 16, finish, (jnp.zeros((8, LANES), F32),) * 9)
        for at in range(9):
            tsum[j, at : at + 1, :] = jnp.sum(sums[at], axis=0, keepdims=True)
        tsum[j, 9:16, :] = jnp.zeros((7, LANES), F32)
        for i in range(2):
            put(i, j, slot).start()
        return 0

    def give(m, d):
        box = (early, late)[m]
        return pltpu.make_async_remote_copy(
            src_ref=box.at[me], dst_ref=box.at[me], send_sem=ts_sem.at[m, d], recv_sem=tr_sem.at[m, d],
            device_id={"ctx": lax.rem(me + d, n)}, device_id_type=MESH,
        )

    cut = max(0, tiles - 2)
    for m, (lo, hi) in enumerate(((0, cut), (cut, tiles))):
        lax.fori_loop(lo, hi, phase2, 0)
        box = (early, late)[m]
        base = 0
        if m == 0:
            high, low = split(gacc[...])
            box[me, 0:modes, :] = high
            box[me, modes : 2 * modes, :] = low
            base = 2 * modes
        for j in range(lo, hi):
            box[me, base + 16 * (j - lo) : base + 16 * (j - lo + 1), :] = tsum[j].astype(BF16)
        for d in range(1, n):
            give(m, d).start()
    for j in range(max(0, tiles - 2), tiles):
        for i in range(2):
            put(i, j, j % 2).wait()
    for m, (lo, hi) in enumerate(((0, cut), (cut, tiles))):
        for d in range(1, n):
            give(m, d).wait()
        box = (early, late)[m]
        total = box[0].astype(F32)
        for s in range(1, n):
            total = total + box[s].astype(F32)
        base = 0
        if m == 0:
            res_out[...] = total[0:modes] + total[modes : 2 * modes]
            base = 2 * modes
        for j in range(lo, hi):
            taps_out[j] = total[base + 16 * (j - lo) : base + 16 * (j - lo + 1)]


def outputs_kernel(
    n, length, groups,
    query, key, value, cot, taps, long_low, back_low, halo, after, rn, wn, sout, gin, taps_sum, res_sum,
    mixed, grad_q, grad_k, grad_v, grad_taps, grad_res,
    uf, ef,
):
    first = lax.axis_index("ctx") == 0
    last = lax.axis_index("ctx") == n - 1
    for i in range(3):
        uf[i, 0:8, :] = jnp.where(first, 0.0, halo[i].astype(F32)[8:16])
        uf[i, 8 + length : 16 + length, :] = jnp.where(last, 0.0, after[i].astype(F32)[0:8])
    streams = (query, key, value)

    def widen(c, _):
        for i in range(3):
            rows = pl.ds(pl.multiple_of(c * 64, 64), 64)
            uf[i, pl.ds(pl.multiple_of(c * 64 + 8, 8), 64), :] = streams[i][rows, :].astype(F32)
        return 0

    lax.fori_loop(0, length // 64, widen, 0)
    tap = [[taps[i, l : l + 1, :] for l in range(3)] for i in range(3)]

    rn_j, wn_j = rn[0], wn[0]
    one = jnp.exp(rn_j)
    less = jnp.exp(-rn_j)

    def over(x):
        return jnp.sum(x, axis=0, keepdims=True)

    short = []
    for i in range(3):
        view = uf.at[i, length : length + 16, :]
        short.append(tap[i][0] * view[8:16, :] + tap[i][1] * view[7:15, :] + tap[i][2] * view[6:14, :])
    cot_next = jnp.where(last, 0.0, after[3].astype(F32)[0:8])
    x_next = (short[1] * short[2]).astype(BF16).astype(F32)[0:2]
    g_next = (cot_next * short[0]).astype(BF16).astype(F32)[0:1]
    h0 = over(wn_j)
    h1 = over(wn_j * less)
    long0 = over(wn_j * less * sout[0]) + h0 * x_next[0:1]
    long1 = over(wn_j * less * less * sout[0]) + h1 * x_next[0:1] + h0 * x_next[1:2]
    gg0 = over(wn_j * one * gin[0])
    gg1 = over(wn_j * one * one * gin[0]) - over(wn_j * one) * g_next
    row8 = row_iota(8)
    long_next = jnp.where(row8 == 0, long0, jnp.where(row8 == 1, long1, 0.0))
    gg_next = jnp.where(row8 == 0, gg0, jnp.where(row8 == 1, gg1, 0.0))
    ef[0, length : length + 8, :] = cot_next * long_next
    ef[1, length : length + 8, :] = gg_next * short[2]
    ef[2, length : length + 8, :] = gg_next * short[1]

    size = 32

    def spread(c, _):
        base = pl.multiple_of(length - size - c * size, size)
        rows = pl.ds(base, size)
        short = []
        for i in range(3):
            view = uf.at[i, pl.ds(base, size + 8), :]
            win = [view[8 - l : 8 + size - l, :] for l in range(3)]
            short.append(tap[i][0] * win[0] + tap[i][1] * win[1] + tap[i][2] * win[2])
        long_here = long_low[0, rows, :].astype(F32)
        back_here = back_low[0, rows, :].astype(F32)
        mixed[rows, :] = (short[0] * long_here).astype(BF16)
        grads = (cot[rows, :].astype(F32) * long_here, back_here * short[2], back_here * short[1])
        for i in range(3):
            ef[i, rows, :] = grads[i]
            view = ef.at[i, pl.ds(base, size + 8), :]
            total = tap[i][0] * grads[i] + tap[i][1] * view[1 : 1 + size, :] + tap[i][2] * view[2 : 2 + size, :]
            (grad_q, grad_k, grad_v)[i][rows, :] = total.astype(BF16)
        return 0

    lax.fori_loop(0, length // size, spread, 0)
    for i in range(3):
        grad_taps[i] = taps_sum[0, 3 * i : 3 * i + 3, :]
    grad_res[...] = res_sum[:, 0:groups]


def local(n, query, key, value, cot, taps, weights, rates):
    length, width = query.shape
    groups, modes = rates.shape
    tiles = width // LANES
    halves = 2 if tiles % 2 == 0 else 1
    per = tiles // halves
    cut = max(0, tiles - 2)
    hbm = pl.BlockSpec(memory_space=pl.ANY)
    vmem = pl.BlockSpec(memory_space=pltpu.VMEM)
    dma = pltpu.SemaphoreType.DMA
    shape = jax.ShapeDtypeStruct
    natural = shape((tiles, modes, LANES), F32)
    tokens3 = shape((tiles, length, LANES), BF16)
    middle = pl.pallas_call(
        functools.partial(filters_kernel, n, tiles, halves, length, modes),
        out_shape=(
            tokens3, tokens3, shape((3, 16, width), BF16), shape((4, 16, width), BF16),
            natural, natural, natural, natural, shape((tiles, 16, LANES), F32), shape((modes, LANES), F32),
        ),
        in_specs=[hbm] * 4 + [vmem] * 3,
        out_specs=[hbm] * 2 + [vmem] * 8,
        scratch_shapes=[
            pltpu.VMEM((4, tiles, length, LANES), BF16),
            pltpu.VMEM((tiles, 3, length + 16, LANES), F32),
            pltpu.VMEM((groups, BLK, LANES), BF16),
            pltpu.VMEM((groups, BLK, LANES), BF16),
            pltpu.VMEM((groups, BLK, 2 * LANES), BF16),
            pltpu.VMEM((groups, BLK, 2 * LANES), BF16),
            pltpu.VMEM((groups, 3 * modes, LANES), BF16),
            pltpu.VMEM((groups, 3 * modes, LANES), BF16),
            pltpu.VMEM((2, groups, modes, LANES), F32),
            pltpu.VMEM((groups, modes, LANES), F32),
            pltpu.VMEM((halves, 2, per, modes, LANES), BF16),
            pltpu.VMEM((halves, n, per, modes, LANES), BF16),
            pltpu.VMEM((3, 16, width), BF16),
            pltpu.VMEM((4, 16, width), BF16),
            pltpu.VMEM((groups, LANES), F32),
            pltpu.VMEM((groups, LANES), F32),
            pltpu.VMEM((modes, LANES), F32),
            pltpu.VMEM((8, BLK, LANES), F32),
            pltpu.VMEM((8, BLK, LANES), F32),
            pltpu.VMEM((2, 2, length, LANES), BF16),
            pltpu.VMEM((tiles, 16, LANES), F32),
            pltpu.VMEM((n, 2 * modes + 16 * cut, LANES), BF16),
            pltpu.VMEM((n, 16 * (tiles - cut), LANES), BF16),
            dma((4, tiles)), dma((7,)), dma((7,)), dma((halves, n)), dma((halves, n)), dma((2, 2)),
            dma((2, n)), dma((2, n)),
        ],
        compiler_params=pltpu.CompilerParams(
            collective_id=0, has_side_effects=True, vmem_limit_bytes=60 * 1024 * 1024
        ),
    )(query, key, value, cot, taps, rates.T, weights.T)

    def stack(*shape):
        return pl.BlockSpec(shape, lambda j: (j, 0, 0))

    def wide(*shape):
        return pl.BlockSpec(shape, lambda j: (0, 0, j))

    tokens = pl.BlockSpec((length, LANES), lambda j: (0, j))
    big = shape((length, width), BF16)
    state = stack(1, modes, LANES)
    *grads, grad_res = pl.pallas_call(
        functools.partial(outputs_kernel, n, length, groups),
        grid=(tiles,),
        out_shape=(big, big, big, big, shape((3, 3, width), F32), shape((modes, groups), F32)),
        in_specs=[
            tokens, tokens, tokens, tokens, wide(3, 3, LANES), stack(1, length, LANES), stack(1, length, LANES),
            wide(3, 16, LANES), wide(4, 16, LANES), state, state, state, state, stack(1, 16, LANES),
            pl.BlockSpec((modes, LANES), lambda j: (0, 0)),
        ],
        out_specs=[tokens] * 4 + [wide(3, 3, LANES), pl.BlockSpec((modes, groups), lambda j: (0, 0))],
        scratch_shapes=[
            pltpu.VMEM((3, length + 16, LANES), F32),
            pltpu.VMEM((3, length + 8, LANES), F32),
        ],
        compiler_params=pltpu.CompilerParams(
            dimension_semantics=("arbitrary",), vmem_limit_bytes=60 * 1024 * 1024
        ),
    )(query, key, value, cot, taps, *middle)
    return (*grads, grad_res.T)


def solution(mesh):
    rows = P("ctx", "tp")
    n = mesh.shape["ctx"]
    return jax.shard_map(
        functools.partial(local, n),
        mesh=mesh,
        in_specs=(rows, rows, rows, rows, P(None, None, "tp"), P("tp", None), P("tp", None)),
        out_specs=(rows, rows, rows, rows, P(None, None, "tp"), P("tp", None)),
        check_vma=False,
    )
```

```python
import functools

import jax
import jax.numpy as jnp
from jax import lax
from jax.experimental import pallas as pl
from jax.experimental.pallas import tpu as pltpu
from jax.sharding import PartitionSpec as P

BLK = 128
LANES = 128
MEM = 16
HI = lax.Precision.HIGHEST
F32 = jnp.float32
BF16 = jnp.bfloat16
MESH = pl.DeviceIdType.MESH


def lane_iota(rows):
    return lax.broadcasted_iota(jnp.int32, (rows, LANES), 1)


def row_iota(rows):
    return lax.broadcasted_iota(jnp.int32, (rows, LANES), 0)


def turn(parts, piece):
    for d in (1, 2, 4):
        pick = (piece // d) % 2 == 1
        parts = [jnp.where(pick, parts[(g - d) % 8], parts[g]) for g in range(8)]
    return parts


def gather_groups(parts):
    piece = lane_iota(parts[0].shape[0]) // MEM
    parts = [pltpu.roll(p, MEM * b, 1) if b else p for b, p in enumerate(parts)]
    return turn([parts[-g % 8] for g in range(8)], piece)


def gather_blocks(parts):
    piece = lane_iota(parts[0].shape[0]) // MEM
    parts = turn([parts[-g % 8] for g in range(8)], piece)
    return [pltpu.roll(p, LANES - MEM * b, 1) if b else p for b, p in enumerate(parts)]


def split(value):
    high = value.astype(BF16)
    low = (value - high.astype(F32)).astype(BF16)
    return high, low


def dot(a, b, dims=((1,), (0,))):
    return lax.dot_general(a, b, (dims, ((), ())), preferred_element_type=F32)


def column(table, g):
    return jnp.broadcast_to(table[:, MEM * g : MEM * g + 1], table.shape)


def filters_kernel(
    n, tiles, halves, length, modes,
    query, key, value, cot, taps, rates, weights,
    long_out, back_out, halo_out, after_out, rn, wn, sout, gin, taps_out, res_out,
    inb, uf, xs, gs, tf, tb, sf, sb, fs, gb, st, rs, halo, after, r3, w3, gacc, yv, zv, stage, tsum, rc, *rest,
):
    early, late = rest[0:2]
    in_sem, hs_sem, hr_sem, ss_sem, sr_sem, out_sem, ts_sem, tr_sem = rest[2:]
    me = lax.axis_index("ctx")
    per = tiles // halves
    barrier = pltpu.get_barrier_semaphore()
    for d in range(1, n):
        pl.semaphore_signal(barrier, inc=1, device_id={"ctx": lax.rem(me + d, n)}, device_id_type=MESH)

    streams = (query, key, value, cot)

    def fetch(i, j):
        return pltpu.make_async_copy(
            streams[i].at[:, pl.ds(pl.multiple_of(j * LANES, LANES), LANES)], inb.at[i, j], in_sem.at[i, j]
        )

    for j in range(tiles):
        for i in range(4):
            fetch(i, j).start()

    def exact(a, b, dims):
        return lax.dot_general(a, b, (dims, ((), ())), precision=HI, preferred_element_type=F32)

    repeat = (lane_iota(modes) % modes == row_iota(modes)).astype(F32)
    for j in range(tiles):
        group = (lane_iota(8 * tiles) // MEM + 8 * j == row_iota(8 * tiles)).astype(F32)
        rn[j] = exact(rates[...], group, ((1,), (0,)))
        wn[j] = exact(weights[...], group, ((1,), (0,)))
    r3[...] = exact(rates[...], repeat, ((0,), (0,)))
    w3[...] = exact(weights[...], repeat, ((0,), (0,)))

    t_row = row_iota(BLK).astype(F32)
    lane_f = lane_iota(modes).astype(F32)
    lane_b = lane_iota(BLK)
    causal = row_iota(BLK) >= lane_iota(BLK)
    anti = row_iota(BLK) <= lane_iota(BLK)

    def build(j, _):
        rn_j = rn[j]
        for g in range(8):
            at = 8 * j + g
            r_row = r3[pl.ds(at, 1), :]
            w_row = w3[pl.ds(at, 1), :]
            r_col = column(rn_j, g)
            rc[at] = r_col
            pad = jnp.zeros((LANES - 3 * modes, LANES), BF16)
            for ref, reach, peer, mask in (
                (tf, t_row + 1.0, lane_f + 1.0, causal),
                (tb, (BLK - 1.0) - t_row, (BLK - 1.0) - lane_f, anti),
            ):
                high, low = split(w_row * jnp.exp(-r_row * reach))
                zero = jnp.zeros_like(high)
                left = jnp.where(lane_b < 2 * modes, high, jnp.where(lane_b < 3 * modes, low, zero))
                v_high, v_low = split(jnp.exp(r_col * peer))
                right = jnp.concatenate([v_high, v_low, v_high, pad], axis=0)
                table = dot(left, right)
                ref[at, :, 0:BLK] = jnp.where(mask, table, 0.0).astype(BF16)
                ref[at, :, BLK : 2 * BLK] = left
        return 0

    lax.fori_loop(0, tiles // 2, build, 0)
    pl.semaphore_wait(barrier, n - 1)

    def behind(i):
        return pltpu.make_async_remote_copy(
            src_ref=streams[i].at[pl.ds(length - 16, 16), :], dst_ref=halo.at[i],
            send_sem=hs_sem.at[i], recv_sem=hr_sem.at[i],
            device_id={"ctx": lax.rem(me + 1, n)}, device_id_type=MESH,
        )

    def ahead(i):
        return pltpu.make_async_remote_copy(
            src_ref=streams[i].at[pl.ds(0, 16), :], dst_ref=after.at[i],
            send_sem=hs_sem.at[3 + i], recv_sem=hr_sem.at[3 + i],
            device_id={"ctx": lax.rem(me + n - 1, n)}, device_id_type=MESH,
        )

    for i in range(3):
        behind(i).start()
    for i in range(4):
        ahead(i).start()

    lax.fori_loop(tiles // 2, tiles, build, 0)

    def arrive(j, _):
        for i in range(4):
            fetch(i, j).wait()

        def widen(c, _):
            for i in range(3):
                rows = pl.ds(pl.multiple_of(c * 64, 64), 64)
                uf[j, i, pl.ds(pl.multiple_of(c * 64 + 8, 8), 64), :] = inb[i, j, rows, :].astype(F32)
            return 0

        lax.fori_loop(0, length // 64, widen, 0)
        return 0

    lax.fori_loop(0, tiles, arrive, 0)
    for i in range(3):
        behind(i).wait()
    for i in range(4):
        ahead(i).wait()
    halo_out[...] = halo[...]
    after_out[...] = after[...]

    first = (me == 0)
    lane16 = lane_iota(modes)

    def phase1(j, _):
        lanes = pl.ds(pl.multiple_of(j * LANES, LANES), LANES)
        for i in range(3):
            prior = halo[i, :, lanes].astype(F32)[8:16]
            uf[j, i, 0:8, :] = jnp.where(first, 0.0, prior)

        tap = [[taps[i, l : l + 1, lanes] for l in range(3)] for i in range(3)]

        def gate(c, _):
            s0 = pl.multiple_of(c * 16, 16)
            forward, backward = [], []
            for b in range(8):
                base = pl.multiple_of(b * BLK + s0, 16)
                short = []
                for i in range(3):
                    view = uf.at[j, i, pl.ds(base, 24), :]
                    total = tap[i][0] * view[8:24, :] + tap[i][1] * view[7:23, :] + tap[i][2] * view[6:22, :]
                    short.append(total)
                forward.append(short[1] * short[2])
                backward.append(inb[3, j, pl.ds(base, 16), :].astype(F32) * short[0])
            for ref, parts in ((xs, forward), (gs, backward)):
                for g, part in enumerate(gather_groups(parts)):
                    ref[8 * j + g, pl.ds(s0, 16), :] = part.astype(BF16)
            return 0

        lax.fori_loop(0, BLK // 16, gate, 0)

        step = jnp.exp(-rn[j] * float(BLK))
        ends, starts = [], []
        for g in range(8):
            at = 8 * j + g
            r_col = rc[at]
            absorb = jnp.concatenate(split(jnp.exp(-r_col * ((BLK - 1.0) - lane_f))), axis=0)
            both = dot(absorb, xs[at])
            ends.append(both[0:modes] + both[modes : 2 * modes])
            emit = jnp.concatenate(split(jnp.exp(-r_col * (lane_f + 1.0))), axis=0)
            both = dot(emit, gs[at])
            starts.append(both[0:modes] + both[modes : 2 * modes])
        ends, starts = gather_blocks(ends), gather_blocks(starts)
        ahead_state = back_state = jnp.zeros((modes, LANES), F32)
        for b in range(8):
            fs[0, j, b] = ahead_state
            ahead_state = step * ahead_state + ends[b]
            gb[j, b] = starts[b]
        for b in range(7, -1, -1):
            fs[1, j, b] = back_state
            back_state = step * back_state + starts[b]
        st[j // per, 0, j % per] = ahead_state.astype(BF16)
        st[j // per, 1, j % per] = back_state.astype(BF16)
        return 0

    def send(h, d):
        return pltpu.make_async_remote_copy(
            src_ref=st.at[h, (me + d) // n], dst_ref=rs.at[h, d],
            send_sem=ss_sem.at[h, d], recv_sem=sr_sem.at[h, d],
            device_id={"ctx": lax.rem(me + d, n)}, device_id_type=MESH,
        )

    for h in range(halves):
        lax.fori_loop(h * per, (h + 1) * per, phase1, 0)
        for d in range(1, n):
            send(h, d).start()

    gacc[...] = jnp.zeros_like(gacc)

    def within(j, _):
        rn_j = rn[j]
        total = gacc[...]
        turned = [gs[8 * j + g].astype(F32).T.astype(BF16) for g in range(8)]
        pairs = [dot(xs[8 * j + g], turned[g]) for g in range(8)]
        pairs = [jnp.where(anti, p, 0.0).astype(BF16) for p in pairs]
        for g in range(8):
            r_col = rc[8 * j + g]
            rise = jnp.concatenate(split(jnp.exp(r_col * lane_f)), axis=0)
            both = dot(rise, pairs[g])
            terms = (both[0:modes] + both[modes : 2 * modes]) * jnp.exp(-r_col * lane_f)
            total = jnp.where(lane16 == 8 * j + g, total + jnp.sum(terms, axis=1, keepdims=True), total)
        gacc[...] = total
        return 0

    lax.fori_loop(0, tiles, within, 0)

    def combine(j, h):
        jj = j - h * per
        rn_j = rn[j]
        whole = jnp.exp(-rn_j * float(length))
        into = jnp.zeros((modes, LANES), F32)
        back = jnp.zeros((modes, LANES), F32)
        for e in range(n - 1, 0, -1):
            into = whole * into + jnp.where(e <= me, rs[h, e, jj].astype(F32), 0.0)
            back = whole * back + jnp.where(e <= n - 1 - me, rs[h, n - e, jj].astype(F32), 0.0)
        sout[j] = whole * into + st[h, 0, jj].astype(F32)
        gin[j] = back
        step = jnp.exp(-rn_j * float(BLK))
        reach_in, reach_back = into, back
        before, behind_ = [None] * 8, [None] * 8
        for b in range(8):
            before[b] = fs[0, j, b] + reach_in
            behind_[7 - b] = fs[1, j, 7 - b] + reach_back
            reach_in = step * reach_in
            reach_back = step * reach_back
        terms = gb[j, 0] * before[0]
        for b in range(1, 8):
            terms = terms + gb[j, b] * before[b]
        group = (row_iota(LANES) // MEM + 8 * j == lane_iota(LANES)).astype(F32)
        gacc[...] += exact(terms, group, ((1,), (0,)))
        for ref, blocks in ((sf, before), (sb, behind_)):
            for g, state in enumerate(gather_groups(blocks)):
                high, low = split(state)
                ref[8 * j + g] = jnp.concatenate([high, low, high], axis=0)
        return h

    for h in range(halves):
        for d in range(1, n):
            send(h, d).wait()
        lax.fori_loop(h * per, (h + 1) * per, combine, h)

    def put(i, j, slot):
        return pltpu.make_async_copy(stage.at[slot, i], (long_out, back_out)[i].at[j], out_sem.at[slot, i])

    pad = jnp.zeros((BLK - 3 * modes, LANES), BF16)

    def phase2(j, _):
        lanes = pl.ds(pl.multiple_of(j * LANES, LANES), LANES)
        slot = j % 2

        @pl.when(j >= 2)
        def _():
            for i in range(2):
                put(i, j - 2, slot).wait()

        for g in range(8):
            at = 8 * j + g
            yv[g] = dot(tf[at], jnp.concatenate([xs[at], sf[at], pad], axis=0))
            zv[g] = dot(tb[at], jnp.concatenate([gs[at], sb[at], pad], axis=0))
        tap = [[taps[i, l : l + 1, lanes] for l in range(3)] for i in range(3)]

        def finish(c, sums):
            s0 = pl.multiple_of(c * 16, 16)
            rows = pl.ds(s0, 16)
            longs = gather_blocks([yv[g, rows, :] for g in range(8)])
            backs = gather_blocks([zv[g, rows, :] for g in range(8)])
            sums = list(sums)
            for b in range(8):
                base = pl.multiple_of(b * BLK + s0, 16)
                short, windows = [], []
                for i in range(3):
                    view = uf.at[j, i, pl.ds(base, 24), :]
                    win = [view[8 - l : 24 - l, :] for l in range(3)]
                    windows.append(win)
                    if i:
                        short.append(tap[i][0] * win[0] + tap[i][1] * win[1] + tap[i][2] * win[2])
                grads = (
                    inb[3, j, pl.ds(base, 16), :].astype(F32) * longs[b],
                    backs[b] * short[1],
                    backs[b] * short[0],
                )
                for i in range(3):
                    for l in range(3):
                        term = grads[i] * windows[i][l]
                        sums[3 * i + l] = sums[3 * i + l] + (term[0:8] + term[8:16])
            for b in range(8):
                rows = pl.ds(pl.multiple_of(b * BLK + s0, 16), 16)
                stage[slot, 0, rows, :] = longs[b].astype(BF16)
                stage[slot, 1, rows, :] = backs[b].astype(BF16)
            return tuple(sums)

        sums = lax.fori_loop(0, BLK // 16, finish, (jnp.zeros((8, LANES), F32),) * 9)
        for at in range(9):
            tsum[j, at : at + 1, :] = jnp.sum(sums[at], axis=0, keepdims=True)
        tsum[j, 9:16, :] = jnp.zeros((7, LANES), F32)
        for i in range(2):
            put(i, j, slot).start()
        return 0

    def give(m, d):
        box = (early, late)[m]
        return pltpu.make_async_remote_copy(
            src_ref=box.at[me], dst_ref=box.at[me], send_sem=ts_sem.at[m, d], recv_sem=tr_sem.at[m, d],
            device_id={"ctx": lax.rem(me + d, n)}, device_id_type=MESH,
        )

    cut = max(0, tiles - 2)
    for m, (lo, hi) in enumerate(((0, cut), (cut, tiles))):
        lax.fori_loop(lo, hi, phase2, 0)
        box = (early, late)[m]
        base = 0
        if m == 0:
            high, low = split(gacc[...])
            box[me, 0:modes, :] = high
            box[me, modes : 2 * modes, :] = low
            base = 2 * modes
        for j in range(lo, hi):
            box[me, base + 16 * (j - lo) : base + 16 * (j - lo + 1), :] = tsum[j].astype(BF16)
        for d in range(1, n):
            give(m, d).start()
    for j in range(max(0, tiles - 2), tiles):
        for i in range(2):
            put(i, j, j % 2).wait()
    for m, (lo, hi) in enumerate(((0, cut), (cut, tiles))):
        for d in range(1, n):
            give(m, d).wait()
        box = (early, late)[m]
        total = box[0].astype(F32)
        for s in range(1, n):
            total = total + box[s].astype(F32)
        base = 0
        if m == 0:
            res_out[...] = total[0:modes] + total[modes : 2 * modes]
            base = 2 * modes
        for j in range(lo, hi):
            taps_out[j] = total[base + 16 * (j - lo) : base + 16 * (j - lo + 1)]


def outputs_kernel(
    n, length, groups,
    query, key, value, cot, taps, long_low, back_low, halo, after, rn, wn, sout, gin, taps_sum, res_sum,
    mixed, grad_q, grad_k, grad_v, grad_taps, grad_res,
    uf, ef,
):
    first = lax.axis_index("ctx") == 0
    last = lax.axis_index("ctx") == n - 1
    for i in range(3):
        uf[i, 0:8, :] = jnp.where(first, 0.0, halo[i].astype(F32)[8:16])
        uf[i, 8 + length : 16 + length, :] = jnp.where(last, 0.0, after[i].astype(F32)[0:8])
    streams = (query, key, value)

    def widen(c, _):
        for i in range(3):
            rows = pl.ds(pl.multiple_of(c * 64, 64), 64)
            uf[i, pl.ds(pl.multiple_of(c * 64 + 8, 8), 64), :] = streams[i][rows, :].astype(F32)
        return 0

    lax.fori_loop(0, length // 64, widen, 0)
    tap = [[taps[i, l : l + 1, :] for l in range(3)] for i in range(3)]

    rn_j, wn_j = rn[0], wn[0]
    one = jnp.exp(rn_j)
    less = jnp.exp(-rn_j)

    def over(x):
        return jnp.sum(x, axis=0, keepdims=True)

    short = []
    for i in range(3):
        view = uf.at[i, length : length + 16, :]
        short.append(tap[i][0] * view[8:16, :] + tap[i][1] * view[7:15, :] + tap[i][2] * view[6:14, :])
    cot_next = jnp.where(last, 0.0, after[3].astype(F32)[0:8])
    x_next = (short[1] * short[2]).astype(BF16).astype(F32)[0:2]
    g_next = (cot_next * short[0]).astype(BF16).astype(F32)[0:1]
    h0 = over(wn_j)
    h1 = over(wn_j * less)
    long0 = over(wn_j * less * sout[0]) + h0 * x_next[0:1]
    long1 = over(wn_j * less * less * sout[0]) + h1 * x_next[0:1] + h0 * x_next[1:2]
    gg0 = over(wn_j * one * gin[0])
    gg1 = over(wn_j * one * one * gin[0]) - over(wn_j * one) * g_next
    row8 = row_iota(8)
    long_next = jnp.where(row8 == 0, long0, jnp.where(row8 == 1, long1, 0.0))
    gg_next = jnp.where(row8 == 0, gg0, jnp.where(row8 == 1, gg1, 0.0))
    ef[0, length : length + 8, :] = cot_next * long_next
    ef[1, length : length + 8, :] = gg_next * short[2]
    ef[2, length : length + 8, :] = gg_next * short[1]

    size = 32

    def spread(c, _):
        base = pl.multiple_of(length - size - c * size, size)
        rows = pl.ds(base, size)
        short = []
        for i in range(3):
            view = uf.at[i, pl.ds(base, size + 8), :]
            win = [view[8 - l : 8 + size - l, :] for l in range(3)]
            short.append(tap[i][0] * win[0] + tap[i][1] * win[1] + tap[i][2] * win[2])
        long_here = long_low[0, rows, :].astype(F32)
        back_here = back_low[0, rows, :].astype(F32)
        mixed[rows, :] = (short[0] * long_here).astype(BF16)
        grads = (cot[rows, :].astype(F32) * long_here, back_here * short[2], back_here * short[1])
        for i in range(3):
            ef[i, rows, :] = grads[i]
            view = ef.at[i, pl.ds(base, size + 8), :]
            total = tap[i][0] * grads[i] + tap[i][1] * view[1 : 1 + size, :] + tap[i][2] * view[2 : 2 + size, :]
            (grad_q, grad_k, grad_v)[i][rows, :] = total.astype(BF16)
        return 0

    lax.fori_loop(0, length // size, spread, 0)
    for i in range(3):
        grad_taps[i] = taps_sum[0, 3 * i : 3 * i + 3, :]
    grad_res[...] = res_sum[:, 0:groups]


def local(n, query, key, value, cot, taps, weights, rates):
    length, width = query.shape
    groups, modes = rates.shape
    tiles = width // LANES
    halves = 2 if tiles % 2 == 0 else 1
    per = tiles // halves
    cut = max(0, tiles - 2)
    hbm = pl.BlockSpec(memory_space=pl.ANY)
    vmem = pl.BlockSpec(memory_space=pltpu.VMEM)
    dma = pltpu.SemaphoreType.DMA
    shape = jax.ShapeDtypeStruct
    natural = shape((tiles, modes, LANES), F32)
    tokens3 = shape((tiles, length, LANES), BF16)
    middle = pl.pallas_call(
        functools.partial(filters_kernel, n, tiles, halves, length, modes),
        out_shape=(
            tokens3, tokens3, shape((3, 16, width), BF16), shape((4, 16, width), BF16),
            natural, natural, natural, natural, shape((tiles, 16, LANES), F32), shape((modes, LANES), F32),
        ),
        in_specs=[hbm] * 4 + [vmem] * 3,
        out_specs=[hbm] * 2 + [vmem] * 8,
        scratch_shapes=[
            pltpu.VMEM((4, tiles, length, LANES), BF16),
            pltpu.VMEM((tiles, 3, length + 16, LANES), F32),
            pltpu.VMEM((groups, BLK, LANES), BF16),
            pltpu.VMEM((groups, BLK, LANES), BF16),
            pltpu.VMEM((groups, BLK, 2 * LANES), BF16),
            pltpu.VMEM((groups, BLK, 2 * LANES), BF16),
            pltpu.VMEM((groups, 3 * modes, LANES), BF16),
            pltpu.VMEM((groups, 3 * modes, LANES), BF16),
            pltpu.VMEM((2, tiles, 8, modes, LANES), F32),
            pltpu.VMEM((tiles, 8, modes, LANES), F32),
            pltpu.VMEM((halves, 2, per, modes, LANES), BF16),
            pltpu.VMEM((halves, n, per, modes, LANES), BF16),
            pltpu.VMEM((3, 16, width), BF16),
            pltpu.VMEM((4, 16, width), BF16),
            pltpu.VMEM((groups, LANES), F32),
            pltpu.VMEM((groups, LANES), F32),
            pltpu.VMEM((modes, LANES), F32),
            pltpu.VMEM((8, BLK, LANES), F32),
            pltpu.VMEM((8, BLK, LANES), F32),
            pltpu.VMEM((2, 2, length, LANES), BF16),
            pltpu.VMEM((tiles, 16, LANES), F32),
            pltpu.VMEM((groups, modes, LANES), F32),
            pltpu.VMEM((n, 2 * modes + 16 * cut, LANES), BF16),
            pltpu.VMEM((n, 16 * (tiles - cut), LANES), BF16),
            dma((4, tiles)), dma((7,)), dma((7,)), dma((halves, n)), dma((halves, n)), dma((2, 2)),
            dma((2, n)), dma((2, n)),
        ],
        compiler_params=pltpu.CompilerParams(
            collective_id=0, has_side_effects=True, vmem_limit_bytes=60 * 1024 * 1024
        ),
    )(query, key, value, cot, taps, rates.T, weights.T)

    def stack(*shape):
        return pl.BlockSpec(shape, lambda j: (j, 0, 0))

    def wide(*shape):
        return pl.BlockSpec(shape, lambda j: (0, 0, j))

    tokens = pl.BlockSpec((length, LANES), lambda j: (0, j))
    big = shape((length, width), BF16)
    state = stack(1, modes, LANES)
    *grads, grad_res = pl.pallas_call(
        functools.partial(outputs_kernel, n, length, groups),
        grid=(tiles,),
        out_shape=(big, big, big, big, shape((3, 3, width), F32), shape((modes, groups), F32)),
        in_specs=[
            tokens, tokens, tokens, tokens, wide(3, 3, LANES), stack(1, length, LANES), stack(1, length, LANES),
            wide(3, 16, LANES), wide(4, 16, LANES), state, state, state, state, stack(1, 16, LANES),
            pl.BlockSpec((modes, LANES), lambda j: (0, 0)),
        ],
        out_specs=[tokens] * 4 + [wide(3, 3, LANES), pl.BlockSpec((modes, groups), lambda j: (0, 0))],
        scratch_shapes=[
            pltpu.VMEM((3, length + 16, LANES), F32),
            pltpu.VMEM((3, length + 8, LANES), F32),
        ],
        compiler_params=pltpu.CompilerParams(
            dimension_semantics=("arbitrary",), vmem_limit_bytes=60 * 1024 * 1024
        ),
    )(query, key, value, cot, taps, *middle)
    return (*grads, grad_res.T)


def solution(mesh):
    rows = P("ctx", "tp")
    n = mesh.shape["ctx"]
    return jax.shard_map(
        functools.partial(local, n),
        mesh=mesh,
        in_specs=(rows, rows, rows, rows, P(None, None, "tp"), P("tp", None), P("tp", None)),
        out_specs=(rows, rows, rows, rows, P(None, None, "tp"), P("tp", None)),
        check_vma=False,
    )
```

```python
import functools

import jax
import jax.numpy as jnp
from jax import lax
from jax.experimental import pallas as pl
from jax.experimental.pallas import tpu as pltpu
from jax.sharding import PartitionSpec as P

BLK = 128
LANES = 128
MEM = 16
HI = lax.Precision.HIGHEST
F32 = jnp.float32
BF16 = jnp.bfloat16
MESH = pl.DeviceIdType.MESH


def lane_iota(rows):
    return lax.broadcasted_iota(jnp.int32, (rows, LANES), 1)


def row_iota(rows):
    return lax.broadcasted_iota(jnp.int32, (rows, LANES), 0)


def turn(parts, piece):
    for d in (1, 2, 4):
        pick = (piece // d) % 2 == 1
        parts = [jnp.where(pick, parts[(g - d) % 8], parts[g]) for g in range(8)]
    return parts


def gather_groups(parts):
    piece = lane_iota(parts[0].shape[0]) // MEM
    parts = [pltpu.roll(p, MEM * b, 1) if b else p for b, p in enumerate(parts)]
    return turn([parts[-g % 8] for g in range(8)], piece)


def gather_blocks(parts):
    piece = lane_iota(parts[0].shape[0]) // MEM
    parts = turn([parts[-g % 8] for g in range(8)], piece)
    return [pltpu.roll(p, LANES - MEM * b, 1) if b else p for b, p in enumerate(parts)]


def split(value):
    high = value.astype(BF16)
    low = (value - high.astype(F32)).astype(BF16)
    return high, low


def dot(a, b, dims=((1,), (0,))):
    return lax.dot_general(a, b, (dims, ((), ())), preferred_element_type=F32)


def column(table, g):
    return jnp.broadcast_to(table[:, MEM * g : MEM * g + 1], table.shape)


def filters_kernel(
    n, tiles, halves, length, modes,
    query, key, value, cot, taps, rates, weights,
    long_out, back_out, prior_out, next_out, taps_out, res_out,
    inb, uf, xs, gs, tf, tb, sf, sb, fs, gb, st, rs, halo, after, r3, w3, gacc, yv, zv, stage, tsum, rc, rn, wn, sout, gin, *rest,
):
    early, late = rest[0:2]
    in_sem, hs_sem, hr_sem, ss_sem, sr_sem, out_sem, ts_sem, tr_sem = rest[2:]
    me = lax.axis_index("ctx")
    per = tiles // halves
    barrier = pltpu.get_barrier_semaphore()
    for d in range(1, n):
        pl.semaphore_signal(barrier, inc=1, device_id={"ctx": lax.rem(me + d, n)}, device_id_type=MESH)

    streams = (query, key, value, cot)

    def fetch(i, j):
        return pltpu.make_async_copy(
            streams[i].at[:, pl.ds(pl.multiple_of(j * LANES, LANES), LANES)], inb.at[i, j], in_sem.at[i, j]
        )

    for j in range(tiles):
        for i in range(4):
            fetch(i, j).start()

    def exact(a, b, dims):
        return lax.dot_general(a, b, (dims, ((), ())), precision=HI, preferred_element_type=F32)

    repeat = (lane_iota(modes) % modes == row_iota(modes)).astype(F32)
    for j in range(tiles):
        group = (lane_iota(8 * tiles) // MEM + 8 * j == row_iota(8 * tiles)).astype(F32)
        rn[j] = exact(rates[...], group, ((1,), (0,)))
        wn[j] = exact(weights[...], group, ((1,), (0,)))
    r3[...] = exact(rates[...], repeat, ((0,), (0,)))
    w3[...] = exact(weights[...], repeat, ((0,), (0,)))

    t_row = row_iota(BLK).astype(F32)
    lane_f = lane_iota(modes).astype(F32)
    lane_b = lane_iota(BLK)
    causal = row_iota(BLK) >= lane_iota(BLK)
    anti = row_iota(BLK) <= lane_iota(BLK)

    def build(j, _):
        rn_j = rn[j]
        for g in range(8):
            at = 8 * j + g
            r_row = r3[pl.ds(at, 1), :]
            w_row = w3[pl.ds(at, 1), :]
            r_col = column(rn_j, g)
            rc[at] = r_col
            pad = jnp.zeros((LANES - 3 * modes, LANES), BF16)
            for ref, reach, peer, mask in (
                (tf, t_row + 1.0, lane_f + 1.0, causal),
                (tb, (BLK - 1.0) - t_row, (BLK - 1.0) - lane_f, anti),
            ):
                high, low = split(w_row * jnp.exp(-r_row * reach))
                zero = jnp.zeros_like(high)
                left = jnp.where(lane_b < 2 * modes, high, jnp.where(lane_b < 3 * modes, low, zero))
                v_high, v_low = split(jnp.exp(r_col * peer))
                right = jnp.concatenate([v_high, v_low, v_high, pad], axis=0)
                table = dot(left, right)
                ref[at, :, 0:BLK] = jnp.where(mask, table, 0.0).astype(BF16)
                ref[at, :, BLK : 2 * BLK] = left
        return 0

    lax.fori_loop(0, tiles // 2, build, 0)
    pl.semaphore_wait(barrier, n - 1)

    def behind(i):
        return pltpu.make_async_remote_copy(
            src_ref=streams[i].at[pl.ds(length - 16, 16), :], dst_ref=halo.at[i],
            send_sem=hs_sem.at[i], recv_sem=hr_sem.at[i],
            device_id={"ctx": lax.rem(me + 1, n)}, device_id_type=MESH,
        )

    def ahead(i):
        return pltpu.make_async_remote_copy(
            src_ref=streams[i].at[pl.ds(0, 16), :], dst_ref=after.at[i],
            send_sem=hs_sem.at[3 + i], recv_sem=hr_sem.at[3 + i],
            device_id={"ctx": lax.rem(me + n - 1, n)}, device_id_type=MESH,
        )

    for i in range(3):
        behind(i).start()
    for i in range(4):
        ahead(i).start()

    lax.fori_loop(tiles // 2, tiles, build, 0)

    def arrive(j, _):
        for i in range(4):
            fetch(i, j).wait()

        def widen(c, _):
            for i in range(3):
                rows = pl.ds(pl.multiple_of(c * 64, 64), 64)
                uf[j, i, pl.ds(pl.multiple_of(c * 64 + 8, 8), 64), :] = inb[i, j, rows, :].astype(F32)
            return 0

        lax.fori_loop(0, length // 64, widen, 0)
        return 0

    lax.fori_loop(0, tiles, arrive, 0)
    def gate_of(j):
        lanes = pl.ds(pl.multiple_of(j * LANES, LANES), LANES)
        tap = [[taps[i, l : l + 1, lanes] for l in range(3)] for i in range(3)]

        def gate(c, _):
            s0 = pl.multiple_of(c * 16, 16)
            forward, backward = [], []
            for b in range(8):
                base = pl.multiple_of(b * BLK + s0, 16)
                short = []
                for i in range(3):
                    view = uf.at[j, i, pl.ds(base, 24), :]
                    total = tap[i][0] * view[8:24, :] + tap[i][1] * view[7:23, :] + tap[i][2] * view[6:22, :]
                    short.append(total)
                forward.append(short[1] * short[2])
                backward.append(inb[3, j, pl.ds(base, 16), :].astype(F32) * short[0])
            for ref, parts in ((xs, forward), (gs, backward)):
                for g, part in enumerate(gather_groups(parts)):
                    ref[8 * j + g, pl.ds(s0, 16), :] = part.astype(BF16)
            return 0

        return gate

    def gates(j, _):
        lax.fori_loop(1, BLK // 16, gate_of(j), 0)
        return 0

    lax.fori_loop(0, tiles, gates, 0)
    for i in range(3):
        behind(i).wait()
    for i in range(4):
        ahead(i).wait()

    first = (me == 0)
    last = (me == n - 1)
    lane16 = lane_iota(modes)

    def phase1(j, _):
        lanes = pl.ds(pl.multiple_of(j * LANES, LANES), LANES)
        for i in range(3):
            prior = halo[i, :, lanes].astype(F32)[8:16]
            prior = jnp.where(first, 0.0, prior)
            uf[j, i, 0:8, :] = prior
            prior_out[j, i] = prior
            uf[j, i, 8 + length : 16 + length, :] = jnp.where(last, 0.0, after[i, :, lanes].astype(F32)[0:8])

        lax.fori_loop(0, 1, gate_of(j), 0)

        step = jnp.exp(-rn[j] * float(BLK))
        ends, starts = [], []
        for g in range(8):
            at = 8 * j + g
            r_col = rc[at]
            absorb = jnp.concatenate(split(jnp.exp(-r_col * ((BLK - 1.0) - lane_f))), axis=0)
            both = dot(absorb, xs[at])
            ends.append(both[0:modes] + both[modes : 2 * modes])
            emit = jnp.concatenate(split(jnp.exp(-r_col * (lane_f + 1.0))), axis=0)
            both = dot(emit, gs[at])
            starts.append(both[0:modes] + both[modes : 2 * modes])
        ends, starts = gather_blocks(ends), gather_blocks(starts)
        ahead_state = back_state = jnp.zeros((modes, LANES), F32)
        for b in range(8):
            fs[0, j, b] = ahead_state
            ahead_state = step * ahead_state + ends[b]
            gb[j, b] = starts[b]
        for b in range(7, -1, -1):
            fs[1, j, b] = back_state
            back_state = step * back_state + starts[b]
        st[j // per, 0, j % per] = ahead_state.astype(BF16)
        st[j // per, 1, j % per] = back_state.astype(BF16)
        return 0

    def send(h, d):
        return pltpu.make_async_remote_copy(
            src_ref=st.at[h, (me + d) // n], dst_ref=rs.at[h, d],
            send_sem=ss_sem.at[h, d], recv_sem=sr_sem.at[h, d],
            device_id={"ctx": lax.rem(me + d, n)}, device_id_type=MESH,
        )

    for h in range(halves):
        lax.fori_loop(h * per, (h + 1) * per, phase1, 0)
        for d in range(1, n):
            send(h, d).start()

    gacc[...] = jnp.zeros_like(gacc)

    def within(j, _):
        rn_j = rn[j]
        total = gacc[...]
        turned = [gs[8 * j + g].astype(F32).T.astype(BF16) for g in range(8)]
        pairs = [dot(xs[8 * j + g], turned[g]) for g in range(8)]
        pairs = [jnp.where(anti, p, 0.0).astype(BF16) for p in pairs]
        for g in range(8):
            r_col = rc[8 * j + g]
            rise = jnp.concatenate(split(jnp.exp(r_col * lane_f)), axis=0)
            both = dot(rise, pairs[g])
            terms = (both[0:modes] + both[modes : 2 * modes]) * jnp.exp(-r_col * lane_f)
            total = jnp.where(lane16 == 8 * j + g, total + jnp.sum(terms, axis=1, keepdims=True), total)
        gacc[...] = total
        return 0

    lax.fori_loop(0, tiles, within, 0)

    def combine(j, h):
        jj = j - h * per
        rn_j = rn[j]
        whole = jnp.exp(-rn_j * float(length))
        into = jnp.zeros((modes, LANES), F32)
        back = jnp.zeros((modes, LANES), F32)
        for e in range(n - 1, 0, -1):
            into = whole * into + jnp.where(e <= me, rs[h, e, jj].astype(F32), 0.0)
            back = whole * back + jnp.where(e <= n - 1 - me, rs[h, n - e, jj].astype(F32), 0.0)
        sout[j] = whole * into + st[h, 0, jj].astype(F32)
        gin[j] = back
        step = jnp.exp(-rn_j * float(BLK))
        reach_in, reach_back = into, back
        before, behind_ = [None] * 8, [None] * 8
        for b in range(8):
            before[b] = fs[0, j, b] + reach_in
            behind_[7 - b] = fs[1, j, 7 - b] + reach_back
            reach_in = step * reach_in
            reach_back = step * reach_back
        terms = gb[j, 0] * before[0]
        for b in range(1, 8):
            terms = terms + gb[j, b] * before[b]
        group = (row_iota(LANES) // MEM + 8 * j == lane_iota(LANES)).astype(F32)
        gacc[...] += exact(terms, group, ((1,), (0,)))
        for ref, blocks in ((sf, before), (sb, behind_)):
            for g, state in enumerate(gather_groups(blocks)):
                high, low = split(state)
                ref[8 * j + g] = jnp.concatenate([high, low, high], axis=0)
        return h


    def put(i, j, slot):
        return pltpu.make_async_copy(stage.at[slot, i], (long_out, back_out)[i].at[j], out_sem.at[slot, i])

    pad = jnp.zeros((BLK - 3 * modes, LANES), BF16)

    def phase2(j, _):
        lanes = pl.ds(pl.multiple_of(j * LANES, LANES), LANES)
        slot = j % 2

        @pl.when(j >= 2)
        def _():
            for i in range(2):
                put(i, j - 2, slot).wait()

        for g in range(8):
            at = 8 * j + g
            yv[g] = dot(tf[at], jnp.concatenate([xs[at], sf[at], pad], axis=0))
            zv[g] = dot(tb[at], jnp.concatenate([gs[at], sb[at], pad], axis=0))
        tap = [[taps[i, l : l + 1, lanes] for l in range(3)] for i in range(3)]

        def finish(c, sums):
            s0 = pl.multiple_of(c * 16, 16)
            rows = pl.ds(s0, 16)
            longs = gather_blocks([yv[g, rows, :] for g in range(8)])
            backs = gather_blocks([zv[g, rows, :] for g in range(8)])
            sums = list(sums)
            for b in range(8):
                base = pl.multiple_of(b * BLK + s0, 16)
                short, windows = [], []
                for i in range(3):
                    view = uf.at[j, i, pl.ds(base, 24), :]
                    win = [view[8 - l : 24 - l, :] for l in range(3)]
                    windows.append(win)
                    if i:
                        short.append(tap[i][0] * win[0] + tap[i][1] * win[1] + tap[i][2] * win[2])
                grads = (
                    inb[3, j, pl.ds(base, 16), :].astype(F32) * longs[b],
                    backs[b] * short[1],
                    backs[b] * short[0],
                )
                for i in range(3):
                    for l in range(3):
                        term = grads[i] * windows[i][l]
                        sums[3 * i + l] = sums[3 * i + l] + (term[0:8] + term[8:16])
            for b in range(8):
                rows = pl.ds(pl.multiple_of(b * BLK + s0, 16), 16)
                stage[slot, 0, rows, :] = longs[b].astype(BF16)
                stage[slot, 1, rows, :] = backs[b].astype(BF16)
            return tuple(sums)

        sums = lax.fori_loop(0, BLK // 16, finish, (jnp.zeros((8, LANES), F32),) * 9)
        for at in range(9):
            tsum[j, at : at + 1, :] = jnp.sum(sums[at], axis=0, keepdims=True)
        tsum[j, 9:16, :] = jnp.zeros((7, LANES), F32)
        for i in range(2):
            put(i, j, slot).start()
        return 0

    def give(m, d):
        box = (early, late)[m]
        return pltpu.make_async_remote_copy(
            src_ref=box.at[me], dst_ref=box.at[me], send_sem=ts_sem.at[m, d], recv_sem=tr_sem.at[m, d],
            device_id={"ctx": lax.rem(me + d, n)}, device_id_type=MESH,
        )

    def absorb_half(h):
        for d in range(1, n):
            send(h, d).wait()
        lax.fori_loop(h * per, (h + 1) * per, combine, h)

    cut = max(0, tiles - 2)
    absorb_half(0)
    if halves == 2:
        lax.fori_loop(0, min(per, cut), phase2, 0)
        absorb_half(1)
    for m, (lo, hi) in enumerate(((0, cut), (cut, tiles))):
        lax.fori_loop(min(per, cut) if m == 0 else lo, hi, phase2, 0)
        box = (early, late)[m]
        base = 0
        if m == 0:
            high, low = split(gacc[...])
            box[me, 0:modes, :] = high
            box[me, modes : 2 * modes, :] = low
            base = 2 * modes
        for j in range(lo, hi):
            box[me, base + 16 * (j - lo) : base + 16 * (j - lo + 1), :] = tsum[j].astype(BF16)
        for d in range(1, n):
            give(m, d).start()
    def follow(j, _):
        lanes = pl.ds(pl.multiple_of(j * LANES, LANES), LANES)
        tap = [[taps[i, l : l + 1, lanes] for l in range(3)] for i in range(3)]

        rn_j, wn_j = rn[j], wn[j]
        one = jnp.exp(rn_j)
        less = jnp.exp(-rn_j)

        def over(x):
            return jnp.sum(x, axis=0, keepdims=True)

        short = []
        for i in range(3):
            view = uf.at[j, i, length : length + 16, :]
            short.append(tap[i][0] * view[8:16, :] + tap[i][1] * view[7:15, :] + tap[i][2] * view[6:14, :])
        cot_next = jnp.where(last, 0.0, after[3, :, lanes].astype(F32)[0:8])
        x_next = (short[1] * short[2]).astype(BF16).astype(F32)[0:2]
        g_next = (cot_next * short[0]).astype(BF16).astype(F32)[0:1]
        h0 = over(wn_j)
        h1 = over(wn_j * less)
        long0 = over(wn_j * less * sout[j]) + h0 * x_next[0:1]
        long1 = over(wn_j * less * less * sout[j]) + h1 * x_next[0:1] + h0 * x_next[1:2]
        gg0 = over(wn_j * one * gin[j])
        gg1 = over(wn_j * one * one * gin[j]) - over(wn_j * one) * g_next
        row8 = row_iota(8)
        long_next = jnp.where(row8 == 0, long0, jnp.where(row8 == 1, long1, 0.0))
        gg_next = jnp.where(row8 == 0, gg0, jnp.where(row8 == 1, gg1, 0.0))
        next_out[j, 0] = cot_next * long_next
        next_out[j, 1] = gg_next * short[2]
        next_out[j, 2] = gg_next * short[1]
        return 0

    lax.fori_loop(0, tiles, follow, 0)
    for j in range(max(0, tiles - 2), tiles):
        for i in range(2):
            put(i, j, j % 2).wait()
    for m, (lo, hi) in enumerate(((0, cut), (cut, tiles))):
        for d in range(1, n):
            give(m, d).wait()
        box = (early, late)[m]
        total = box[0].astype(F32)
        for s in range(1, n):
            total = total + box[s].astype(F32)
        base = 0
        if m == 0:
            res_out[...] = total[0:modes] + total[modes : 2 * modes]
            base = 2 * modes
        for j in range(lo, hi):
            taps_out[j] = total[base + 16 * (j - lo) : base + 16 * (j - lo + 1)]


def outputs_kernel(
    length, groups,
    query, key, value, cot, taps, long_low, back_low, prior, following, taps_sum, res_sum,
    mixed, grad_q, grad_k, grad_v, grad_taps, grad_res,
    uf, ef,
):
    for i in range(3):
        uf[i, 0:8, :] = prior[0, i]
        ef[i, length : length + 8, :] = following[0, i]
    streams = (query, key, value)

    def widen(c, _):
        for i in range(3):
            rows = pl.ds(pl.multiple_of(c * 64, 64), 64)
            uf[i, pl.ds(pl.multiple_of(c * 64 + 8, 8), 64), :] = streams[i][rows, :].astype(F32)
        return 0

    lax.fori_loop(0, length // 64, widen, 0)
    tap = [[taps[i, l : l + 1, :] for l in range(3)] for i in range(3)]

    size = 64

    def spread(c, _):
        base = pl.multiple_of(length - size - c * size, size)
        rows = pl.ds(base, size)
        short = []
        for i in range(3):
            view = uf.at[i, pl.ds(base, size + 8), :]
            win = [view[8 - l : 8 + size - l, :] for l in range(3)]
            short.append(tap[i][0] * win[0] + tap[i][1] * win[1] + tap[i][2] * win[2])
        long_here = long_low[0, rows, :].astype(F32)
        back_here = back_low[0, rows, :].astype(F32)
        mixed[rows, :] = (short[0] * long_here).astype(BF16)
        grads = (cot[rows, :].astype(F32) * long_here, back_here * short[2], back_here * short[1])
        for i in range(3):
            ef[i, rows, :] = grads[i]
            view = ef.at[i, pl.ds(base, size + 8), :]
            total = tap[i][0] * grads[i] + tap[i][1] * view[1 : 1 + size, :] + tap[i][2] * view[2 : 2 + size, :]
            (grad_q, grad_k, grad_v)[i][rows, :] = total.astype(BF16)
        return 0

    lax.fori_loop(0, length // size, spread, 0)
    for i in range(3):
        grad_taps[i] = taps_sum[0, 3 * i : 3 * i + 3, :]
    grad_res[...] = res_sum[:, 0:groups]


def local(n, query, key, value, cot, taps, weights, rates):
    length, width = query.shape
    groups, modes = rates.shape
    tiles = width // LANES
    halves = 2 if tiles % 2 == 0 else 1
    per = tiles // halves
    cut = max(0, tiles - 2)
    hbm = pl.BlockSpec(memory_space=pl.ANY)
    vmem = pl.BlockSpec(memory_space=pltpu.VMEM)
    dma = pltpu.SemaphoreType.DMA
    shape = jax.ShapeDtypeStruct
    edge = shape((tiles, 3, 8, LANES), F32)
    tokens3 = shape((tiles, length, LANES), BF16)
    middle = pl.pallas_call(
        functools.partial(filters_kernel, n, tiles, halves, length, modes),
        out_shape=(
            tokens3, tokens3, edge, edge, shape((tiles, 16, LANES), F32), shape((modes, LANES), F32),
        ),
        in_specs=[hbm] * 4 + [vmem] * 3,
        out_specs=[hbm] * 2 + [vmem] * 4,
        scratch_shapes=[
            pltpu.VMEM((4, tiles, length, LANES), BF16),
            pltpu.VMEM((tiles, 3, length + 16, LANES), F32),
            pltpu.VMEM((groups, BLK, LANES), BF16),
            pltpu.VMEM((groups, BLK, LANES), BF16),
            pltpu.VMEM((groups, BLK, 2 * LANES), BF16),
            pltpu.VMEM((groups, BLK, 2 * LANES), BF16),
            pltpu.VMEM((groups, 3 * modes, LANES), BF16),
            pltpu.VMEM((groups, 3 * modes, LANES), BF16),
            pltpu.VMEM((2, tiles, 8, modes, LANES), F32),
            pltpu.VMEM((tiles, 8, modes, LANES), F32),
            pltpu.VMEM((halves, 2, per, modes, LANES), BF16),
            pltpu.VMEM((halves, n, per, modes, LANES), BF16),
            pltpu.VMEM((3, 16, width), BF16),
            pltpu.VMEM((4, 16, width), BF16),
            pltpu.VMEM((groups, LANES), F32),
            pltpu.VMEM((groups, LANES), F32),
            pltpu.VMEM((modes, LANES), F32),
            pltpu.VMEM((8, BLK, LANES), F32),
            pltpu.VMEM((8, BLK, LANES), F32),
            pltpu.VMEM((2, 2, length, LANES), BF16),
            pltpu.VMEM((tiles, 16, LANES), F32),
            pltpu.VMEM((groups, modes, LANES), F32),
            pltpu.VMEM((tiles, modes, LANES), F32),
            pltpu.VMEM((tiles, modes, LANES), F32),
            pltpu.VMEM((tiles, modes, LANES), F32),
            pltpu.VMEM((tiles, modes, LANES), F32),
            pltpu.VMEM((n, 2 * modes + 16 * cut, LANES), BF16),
            pltpu.VMEM((n, 16 * (tiles - cut), LANES), BF16),
            dma((4, tiles)), dma((7,)), dma((7,)), dma((halves, n)), dma((halves, n)), dma((2, 2)),
            dma((2, n)), dma((2, n)),
        ],
        compiler_params=pltpu.CompilerParams(
            collective_id=0, has_side_effects=True, vmem_limit_bytes=60 * 1024 * 1024
        ),
    )(query, key, value, cot, taps, rates.T, weights.T)

    def stack(*shape):
        return pl.BlockSpec(shape, lambda j: (j, 0, 0))

    def wide(*shape):
        return pl.BlockSpec(shape, lambda j: (0, 0, j))

    tokens = pl.BlockSpec((length, LANES), lambda j: (0, j))
    big = shape((length, width), BF16)
    edges = pl.BlockSpec((1, 3, 8, LANES), lambda j: (j, 0, 0, 0))
    *grads, grad_res = pl.pallas_call(
        functools.partial(outputs_kernel, length, groups),
        grid=(tiles,),
        out_shape=(big, big, big, big, shape((3, 3, width), F32), shape((modes, groups), F32)),
        in_specs=[
            tokens, tokens, tokens, tokens, wide(3, 3, LANES), stack(1, length, LANES), stack(1, length, LANES),
            edges, edges, stack(1, 16, LANES),
            pl.BlockSpec((modes, LANES), lambda j: (0, 0)),
        ],
        out_specs=[tokens] * 4 + [wide(3, 3, LANES), pl.BlockSpec((modes, groups), lambda j: (0, 0))],
        scratch_shapes=[
            pltpu.VMEM((3, length + 16, LANES), F32),
            pltpu.VMEM((3, length + 8, LANES), F32),
        ],
        compiler_params=pltpu.CompilerParams(
            dimension_semantics=("arbitrary",), vmem_limit_bytes=60 * 1024 * 1024
        ),
    )(query, key, value, cot, taps, *middle)
    return (*grads, grad_res.T)


def solution(mesh):
    rows = P("ctx", "tp")
    n = mesh.shape["ctx"]
    return jax.shard_map(
        functools.partial(local, n),
        mesh=mesh,
        in_specs=(rows, rows, rows, rows, P(None, None, "tp"), P("tp", None), P("tp", None)),
        out_specs=(rows, rows, rows, rows, P(None, None, "tp"), P("tp", None)),
        check_vma=False,
    )
```

```python
import functools

import jax
import jax.numpy as jnp
from jax import lax
from jax.experimental import pallas as pl
from jax.experimental.pallas import tpu as pltpu
from jax.sharding import PartitionSpec as P

BLK = 128
LANES = 128
MEM = 16
HI = lax.Precision.HIGHEST
F32 = jnp.float32
BF16 = jnp.bfloat16
MESH = pl.DeviceIdType.MESH


def lane_iota(rows):
    return lax.broadcasted_iota(jnp.int32, (rows, LANES), 1)


def row_iota(rows):
    return lax.broadcasted_iota(jnp.int32, (rows, LANES), 0)


def turn(parts, piece):
    for d in (1, 2, 4):
        pick = (piece // d) % 2 == 1
        parts = [jnp.where(pick, parts[(g - d) % 8], parts[g]) for g in range(8)]
    return parts


def gather_groups(parts):
    piece = lane_iota(parts[0].shape[0]) // MEM
    parts = [pltpu.roll(p, MEM * b, 1) if b else p for b, p in enumerate(parts)]
    return turn([parts[-g % 8] for g in range(8)], piece)


def gather_blocks(parts):
    piece = lane_iota(parts[0].shape[0]) // MEM
    parts = turn([parts[-g % 8] for g in range(8)], piece)
    return [pltpu.roll(p, LANES - MEM * b, 1) if b else p for b, p in enumerate(parts)]


def split(value):
    high = value.astype(BF16)
    low = (value - high.astype(F32)).astype(BF16)
    return high, low


def dot(a, b, dims=((1,), (0,))):
    return lax.dot_general(a, b, (dims, ((), ())), preferred_element_type=F32)


def column(table, g):
    return jnp.broadcast_to(table[:, MEM * g : MEM * g + 1], table.shape)


def filters_kernel(
    n, tiles, halves, length, modes,
    query, key, value, cot, taps, rates, weights,
    long_out, back_out, prior_out, next_out, taps_out, res_out,
    inb, uf, xs, gs, tf, tb, sf, sb, fs, gb, st, rs, halo, after, r3, w3, gacc, yv, zv, stage, tsum, rc, rn, wn, sout, gin, *rest,
):
    early, late = rest[0:2]
    in_sem, hs_sem, hr_sem, ss_sem, sr_sem, out_sem, ts_sem, tr_sem = rest[2:]
    me = lax.axis_index("ctx")
    per = tiles // halves
    barrier = pltpu.get_barrier_semaphore()
    for d in range(1, n):
        pl.semaphore_signal(barrier, inc=1, device_id={"ctx": lax.rem(me + d, n)}, device_id_type=MESH)

    streams = (query, key, value, cot)

    def fetch(i, j):
        return pltpu.make_async_copy(
            streams[i].at[:, pl.ds(pl.multiple_of(j * LANES, LANES), LANES)], inb.at[i, j], in_sem.at[i, j]
        )

    for j in range(tiles):
        for i in range(4):
            fetch(i, j).start()

    def exact(a, b, dims):
        return lax.dot_general(a, b, (dims, ((), ())), precision=HI, preferred_element_type=F32)

    repeat = (lane_iota(modes) % modes == row_iota(modes)).astype(F32)
    for j in range(tiles):
        group = (lane_iota(8 * tiles) // MEM + 8 * j == row_iota(8 * tiles)).astype(F32)
        rn[j] = exact(rates[...], group, ((1,), (0,)))
        wn[j] = exact(weights[...], group, ((1,), (0,)))
    r3[...] = exact(rates[...], repeat, ((0,), (0,)))
    w3[...] = exact(weights[...], repeat, ((0,), (0,)))

    t_row = row_iota(BLK).astype(F32)
    lane_f = lane_iota(modes).astype(F32)
    lane_b = lane_iota(BLK)
    causal = row_iota(BLK) >= lane_iota(BLK)
    anti = row_iota(BLK) <= lane_iota(BLK)

    def build(j, _):
        rn_j = rn[j]
        for g in range(8):
            at = 8 * j + g
            r_row = r3[pl.ds(at, 1), :]
            w_row = w3[pl.ds(at, 1), :]
            r_col = column(rn_j, g)
            rc[at] = r_col
            pad = jnp.zeros((LANES - 3 * modes, LANES), BF16)
            for ref, reach, peer, mask in (
                (tf, t_row + 1.0, lane_f + 1.0, causal),
                (tb, (BLK - 1.0) - t_row, (BLK - 1.0) - lane_f, anti),
            ):
                high, low = split(w_row * jnp.exp(-r_row * reach))
                zero = jnp.zeros_like(high)
                left = jnp.where(lane_b < 2 * modes, high, jnp.where(lane_b < 3 * modes, low, zero))
                v_high, v_low = split(jnp.exp(r_col * peer))
                right = jnp.concatenate([v_high, v_low, v_high, pad], axis=0)
                table = dot(left, right)
                ref[at, :, 0:BLK] = jnp.where(mask, table, 0.0).astype(BF16)
                ref[at, :, BLK : 2 * BLK] = left
        return 0

    lax.fori_loop(0, tiles // 2, build, 0, unroll=2)
    pl.semaphore_wait(barrier, n - 1)

    def behind(i):
        return pltpu.make_async_remote_copy(
            src_ref=streams[i].at[pl.ds(length - 16, 16), :], dst_ref=halo.at[i],
            send_sem=hs_sem.at[i], recv_sem=hr_sem.at[i],
            device_id={"ctx": lax.rem(me + 1, n)}, device_id_type=MESH,
        )

    def ahead(i):
        return pltpu.make_async_remote_copy(
            src_ref=streams[i].at[pl.ds(0, 16), :], dst_ref=after.at[i],
            send_sem=hs_sem.at[3 + i], recv_sem=hr_sem.at[3 + i],
            device_id={"ctx": lax.rem(me + n - 1, n)}, device_id_type=MESH,
        )

    for i in range(3):
        behind(i).start()
    for i in range(4):
        ahead(i).start()

    lax.fori_loop(tiles // 2, tiles, build, 0, unroll=2)

    def arrive(j, _):
        for i in range(4):
            fetch(i, j).wait()

        def widen(c, _):
            for i in range(3):
                rows = pl.ds(pl.multiple_of(c * 64, 64), 64)
                uf[j, i, pl.ds(pl.multiple_of(c * 64 + 8, 8), 64), :] = inb[i, j, rows, :].astype(F32)
            return 0

        lax.fori_loop(0, length // 64, widen, 0)
        return 0

    lax.fori_loop(0, tiles, arrive, 0)
    def gate_of(j):
        lanes = pl.ds(pl.multiple_of(j * LANES, LANES), LANES)
        tap = [[taps[i, l : l + 1, lanes] for l in range(3)] for i in range(3)]

        def gate(c, _):
            s0 = pl.multiple_of(c * 16, 16)
            forward, backward = [], []
            for b in range(8):
                base = pl.multiple_of(b * BLK + s0, 16)
                short = []
                for i in range(3):
                    view = uf.at[j, i, pl.ds(base, 24), :]
                    total = tap[i][0] * view[8:24, :] + tap[i][1] * view[7:23, :] + tap[i][2] * view[6:22, :]
                    short.append(total)
                forward.append(short[1] * short[2])
                backward.append(inb[3, j, pl.ds(base, 16), :].astype(F32) * short[0])
            for ref, parts in ((xs, forward), (gs, backward)):
                for g, part in enumerate(gather_groups(parts)):
                    ref[8 * j + g, pl.ds(s0, 16), :] = part.astype(BF16)
            return 0

        return gate

    def gates(j, _):
        lax.fori_loop(1, BLK // 16, gate_of(j), 0, unroll=7)
        return 0

    lax.fori_loop(0, tiles, gates, 0)
    for i in range(3):
        behind(i).wait()
    for i in range(4):
        ahead(i).wait()

    first = (me == 0)
    last = (me == n - 1)
    lane16 = lane_iota(modes)

    def phase1(j, _):
        lanes = pl.ds(pl.multiple_of(j * LANES, LANES), LANES)
        for i in range(3):
            prior = halo[i, :, lanes].astype(F32)[8:16]
            prior = jnp.where(first, 0.0, prior)
            uf[j, i, 0:8, :] = prior
            prior_out[j, i] = prior
            uf[j, i, 8 + length : 16 + length, :] = jnp.where(last, 0.0, after[i, :, lanes].astype(F32)[0:8])

        lax.fori_loop(0, 1, gate_of(j), 0)

        step = jnp.exp(-rn[j] * float(BLK))
        ends, starts = [], []
        for g in range(8):
            at = 8 * j + g
            r_col = rc[at]
            absorb = jnp.concatenate(split(jnp.exp(-r_col * ((BLK - 1.0) - lane_f))), axis=0)
            both = dot(absorb, xs[at])
            ends.append(both[0:modes] + both[modes : 2 * modes])
            emit = jnp.concatenate(split(jnp.exp(-r_col * (lane_f + 1.0))), axis=0)
            both = dot(emit, gs[at])
            starts.append(both[0:modes] + both[modes : 2 * modes])
        ends, starts = gather_blocks(ends), gather_blocks(starts)
        ahead_state = back_state = jnp.zeros((modes, LANES), F32)
        for b in range(8):
            fs[0, j, b] = ahead_state
            ahead_state = step * ahead_state + ends[b]
            gb[j, b] = starts[b]
        for b in range(7, -1, -1):
            fs[1, j, b] = back_state
            back_state = step * back_state + starts[b]
        st[j // per, 0, j % per] = ahead_state.astype(BF16)
        st[j // per, 1, j % per] = back_state.astype(BF16)
        return 0

    def send(h, d):
        return pltpu.make_async_remote_copy(
            src_ref=st.at[h, (me + d) // n], dst_ref=rs.at[h, d],
            send_sem=ss_sem.at[h, d], recv_sem=sr_sem.at[h, d],
            device_id={"ctx": lax.rem(me + d, n)}, device_id_type=MESH,
        )

    for h in range(halves):
        lax.fori_loop(h * per, (h + 1) * per, phase1, 0)
        for d in range(1, n):
            send(h, d).start()

    gacc[...] = jnp.zeros_like(gacc)

    def within(j, _):
        rn_j = rn[j]
        total = gacc[...]
        turned = [gs[8 * j + g].astype(F32).T.astype(BF16) for g in range(8)]
        pairs = [dot(xs[8 * j + g], turned[g]) for g in range(8)]
        pairs = [jnp.where(anti, p, 0.0).astype(BF16) for p in pairs]
        for g in range(8):
            r_col = rc[8 * j + g]
            rise = jnp.concatenate(split(jnp.exp(r_col * lane_f)), axis=0)
            both = dot(rise, pairs[g])
            terms = (both[0:modes] + both[modes : 2 * modes]) * jnp.exp(-r_col * lane_f)
            total = jnp.where(lane16 == 8 * j + g, total + jnp.sum(terms, axis=1, keepdims=True), total)
        gacc[...] = total
        return 0

    lax.fori_loop(0, tiles, within, 0, unroll=2)

    def combine(j, h):
        jj = j - h * per
        rn_j = rn[j]
        whole = jnp.exp(-rn_j * float(length))
        into = jnp.zeros((modes, LANES), F32)
        back = jnp.zeros((modes, LANES), F32)
        for e in range(n - 1, 0, -1):
            into = whole * into + jnp.where(e <= me, rs[h, e, jj].astype(F32), 0.0)
            back = whole * back + jnp.where(e <= n - 1 - me, rs[h, n - e, jj].astype(F32), 0.0)
        sout[j] = whole * into + st[h, 0, jj].astype(F32)
        gin[j] = back
        step = jnp.exp(-rn_j * float(BLK))
        reach_in, reach_back = into, back
        before, behind_ = [None] * 8, [None] * 8
        for b in range(8):
            before[b] = fs[0, j, b] + reach_in
            behind_[7 - b] = fs[1, j, 7 - b] + reach_back
            reach_in = step * reach_in
            reach_back = step * reach_back
        terms = gb[j, 0] * before[0]
        for b in range(1, 8):
            terms = terms + gb[j, b] * before[b]
        group = (row_iota(LANES) // MEM + 8 * j == lane_iota(LANES)).astype(F32)
        gacc[...] += exact(terms, group, ((1,), (0,)))
        for ref, blocks in ((sf, before), (sb, behind_)):
            for g, state in enumerate(gather_groups(blocks)):
                high, low = split(state)
                ref[8 * j + g] = jnp.concatenate([high, low, high], axis=0)
        return h


    def put(i, j, slot):
        return pltpu.make_async_copy(stage.at[slot, i], (long_out, back_out)[i].at[j], out_sem.at[slot, i])

    pad = jnp.zeros((BLK - 3 * modes, LANES), BF16)

    def phase2(j, _):
        lanes = pl.ds(pl.multiple_of(j * LANES, LANES), LANES)
        slot = j % 2

        @pl.when(j >= 2)
        def _():
            for i in range(2):
                put(i, j - 2, slot).wait()

        for g in range(8):
            at = 8 * j + g
            yv[g] = dot(tf[at], jnp.concatenate([xs[at], sf[at], pad], axis=0))
            zv[g] = dot(tb[at], jnp.concatenate([gs[at], sb[at], pad], axis=0))
        tap = [[taps[i, l : l + 1, lanes] for l in range(3)] for i in range(3)]

        def finish(c, sums):
            s0 = pl.multiple_of(c * 16, 16)
            rows = pl.ds(s0, 16)
            longs = gather_blocks([yv[g, rows, :] for g in range(8)])
            backs = gather_blocks([zv[g, rows, :] for g in range(8)])
            sums = list(sums)
            for b in range(8):
                base = pl.multiple_of(b * BLK + s0, 16)
                short, windows = [], []
                for i in range(3):
                    view = uf.at[j, i, pl.ds(base, 24), :]
                    win = [view[8 - l : 24 - l, :] for l in range(3)]
                    windows.append(win)
                    if i:
                        short.append(tap[i][0] * win[0] + tap[i][1] * win[1] + tap[i][2] * win[2])
                grads = (
                    inb[3, j, pl.ds(base, 16), :].astype(F32) * longs[b],
                    backs[b] * short[1],
                    backs[b] * short[0],
                )
                for i in range(3):
                    for l in range(3):
                        term = grads[i] * windows[i][l]
                        sums[3 * i + l] = sums[3 * i + l] + (term[0:8] + term[8:16])
            for b in range(8):
                rows = pl.ds(pl.multiple_of(b * BLK + s0, 16), 16)
                stage[slot, 0, rows, :] = longs[b].astype(BF16)
                stage[slot, 1, rows, :] = backs[b].astype(BF16)
            return tuple(sums)

        sums = lax.fori_loop(0, BLK // 16, finish, (jnp.zeros((8, LANES), F32),) * 9, unroll=4)
        for at in range(9):
            tsum[j, at : at + 1, :] = jnp.sum(sums[at], axis=0, keepdims=True)
        tsum[j, 9:16, :] = jnp.zeros((7, LANES), F32)
        for i in range(2):
            put(i, j, slot).start()
        return 0

    def give(m, d):
        box = (early, late)[m]
        return pltpu.make_async_remote_copy(
            src_ref=box.at[me], dst_ref=box.at[me], send_sem=ts_sem.at[m, d], recv_sem=tr_sem.at[m, d],
            device_id={"ctx": lax.rem(me + d, n)}, device_id_type=MESH,
        )

    def absorb_half(h):
        for d in range(1, n):
            send(h, d).wait()
        lax.fori_loop(h * per, (h + 1) * per, combine, h)

    cut = max(0, tiles - 2)
    absorb_half(0)
    if halves == 2:
        lax.fori_loop(0, min(per, cut), phase2, 0)
        absorb_half(1)
    for m, (lo, hi) in enumerate(((0, cut), (cut, tiles))):
        lax.fori_loop(min(per, cut) if m == 0 else lo, hi, phase2, 0)
        box = (early, late)[m]
        base = 0
        if m == 0:
            high, low = split(gacc[...])
            box[me, 0:modes, :] = high
            box[me, modes : 2 * modes, :] = low
            base = 2 * modes
        for j in range(lo, hi):
            box[me, base + 16 * (j - lo) : base + 16 * (j - lo + 1), :] = tsum[j].astype(BF16)
        for d in range(1, n):
            give(m, d).start()
    def follow(j, _):
        lanes = pl.ds(pl.multiple_of(j * LANES, LANES), LANES)
        tap = [[taps[i, l : l + 1, lanes] for l in range(3)] for i in range(3)]

        rn_j, wn_j = rn[j], wn[j]
        one = jnp.exp(rn_j)
        less = jnp.exp(-rn_j)

        def over(x):
            return jnp.sum(x, axis=0, keepdims=True)

        short = []
        for i in range(3):
            view = uf.at[j, i, length : length + 16, :]
            short.append(tap[i][0] * view[8:16, :] + tap[i][1] * view[7:15, :] + tap[i][2] * view[6:14, :])
        cot_next = jnp.where(last, 0.0, after[3, :, lanes].astype(F32)[0:8])
        x_next = (short[1] * short[2]).astype(BF16).astype(F32)[0:2]
        g_next = (cot_next * short[0]).astype(BF16).astype(F32)[0:1]
        h0 = over(wn_j)
        h1 = over(wn_j * less)
        long0 = over(wn_j * less * sout[j]) + h0 * x_next[0:1]
        long1 = over(wn_j * less * less * sout[j]) + h1 * x_next[0:1] + h0 * x_next[1:2]
        gg0 = over(wn_j * one * gin[j])
        gg1 = over(wn_j * one * one * gin[j]) - over(wn_j * one) * g_next
        row8 = row_iota(8)
        long_next = jnp.where(row8 == 0, long0, jnp.where(row8 == 1, long1, 0.0))
        gg_next = jnp.where(row8 == 0, gg0, jnp.where(row8 == 1, gg1, 0.0))
        next_out[j, 0] = cot_next * long_next
        next_out[j, 1] = gg_next * short[2]
        next_out[j, 2] = gg_next * short[1]
        return 0

    lax.fori_loop(0, tiles, follow, 0)
    for j in range(max(0, tiles - 2), tiles):
        for i in range(2):
            put(i, j, j % 2).wait()
    for m, (lo, hi) in enumerate(((0, cut), (cut, tiles))):
        for d in range(1, n):
            give(m, d).wait()
        box = (early, late)[m]
        total = box[0].astype(F32)
        for s in range(1, n):
            total = total + box[s].astype(F32)
        base = 0
        if m == 0:
            res_out[...] = total[0:modes] + total[modes : 2 * modes]
            base = 2 * modes
        for j in range(lo, hi):
            taps_out[j] = total[base + 16 * (j - lo) : base + 16 * (j - lo + 1)]


def outputs_kernel(
    length, groups,
    query, key, value, cot, taps, long_low, back_low, prior, following, taps_sum, res_sum,
    mixed, grad_q, grad_k, grad_v, grad_taps, grad_res,
    uf, ef,
):
    for i in range(3):
        uf[i, 0:8, :] = prior[0, i]
        ef[i, length : length + 8, :] = following[0, i]
    streams = (query, key, value)

    def widen(c, _):
        for i in range(3):
            rows = pl.ds(pl.multiple_of(c * 64, 64), 64)
            uf[i, pl.ds(pl.multiple_of(c * 64 + 8, 8), 64), :] = streams[i][rows, :].astype(F32)
        return 0

    lax.fori_loop(0, length // 64, widen, 0)
    tap = [[taps[i, l : l + 1, :] for l in range(3)] for i in range(3)]

    size = 64

    def spread(c, _):
        base = pl.multiple_of(length - size - c * size, size)
        rows = pl.ds(base, size)
        short = []
        for i in range(3):
            view = uf.at[i, pl.ds(base, size + 8), :]
            win = [view[8 - l : 8 + size - l, :] for l in range(3)]
            short.append(tap[i][0] * win[0] + tap[i][1] * win[1] + tap[i][2] * win[2])
        long_here = long_low[0, rows, :].astype(F32)
        back_here = back_low[0, rows, :].astype(F32)
        mixed[rows, :] = (short[0] * long_here).astype(BF16)
        grads = (cot[rows, :].astype(F32) * long_here, back_here * short[2], back_here * short[1])
        for i in range(3):
            ef[i, rows, :] = grads[i]
            view = ef.at[i, pl.ds(base, size + 8), :]
            total = tap[i][0] * grads[i] + tap[i][1] * view[1 : 1 + size, :] + tap[i][2] * view[2 : 2 + size, :]
            (grad_q, grad_k, grad_v)[i][rows, :] = total.astype(BF16)
        return 0

    lax.fori_loop(0, length // size, spread, 0, unroll=4)
    for i in range(3):
        grad_taps[i] = taps_sum[0, 3 * i : 3 * i + 3, :]
    grad_res[...] = res_sum[:, 0:groups]


def local(n, query, key, value, cot, taps, weights, rates):
    length, width = query.shape
    groups, modes = rates.shape
    tiles = width // LANES
    halves = 2 if tiles % 2 == 0 else 1
    per = tiles // halves
    cut = max(0, tiles - 2)
    hbm = pl.BlockSpec(memory_space=pl.ANY)
    vmem = pl.BlockSpec(memory_space=pltpu.VMEM)
    dma = pltpu.SemaphoreType.DMA
    shape = jax.ShapeDtypeStruct
    edge = shape((tiles, 3, 8, LANES), F32)
    tokens3 = shape((tiles, length, LANES), BF16)
    middle = pl.pallas_call(
        functools.partial(filters_kernel, n, tiles, halves, length, modes),
        out_shape=(
            tokens3, tokens3, edge, edge, shape((tiles, 16, LANES), F32), shape((modes, LANES), F32),
        ),
        in_specs=[hbm] * 4 + [vmem] * 3,
        out_specs=[hbm] * 2 + [vmem] * 4,
        scratch_shapes=[
            pltpu.VMEM((4, tiles, length, LANES), BF16),
            pltpu.VMEM((tiles, 3, length + 16, LANES), F32),
            pltpu.VMEM((groups, BLK, LANES), BF16),
            pltpu.VMEM((groups, BLK, LANES), BF16),
            pltpu.VMEM((groups, BLK, 2 * LANES), BF16),
            pltpu.VMEM((groups, BLK, 2 * LANES), BF16),
            pltpu.VMEM((groups, 3 * modes, LANES), BF16),
            pltpu.VMEM((groups, 3 * modes, LANES), BF16),
            pltpu.VMEM((2, tiles, 8, modes, LANES), F32),
            pltpu.VMEM((tiles, 8, modes, LANES), F32),
            pltpu.VMEM((halves, 2, per, modes, LANES), BF16),
            pltpu.VMEM((halves, n, per, modes, LANES), BF16),
            pltpu.VMEM((3, 16, width), BF16),
            pltpu.VMEM((4, 16, width), BF16),
            pltpu.VMEM((groups, LANES), F32),
            pltpu.VMEM((groups, LANES), F32),
            pltpu.VMEM((modes, LANES), F32),
            pltpu.VMEM((8, BLK, LANES), F32),
            pltpu.VMEM((8, BLK, LANES), F32),
            pltpu.VMEM((2, 2, length, LANES), BF16),
            pltpu.VMEM((tiles, 16, LANES), F32),
            pltpu.VMEM((groups, modes, LANES), F32),
            pltpu.VMEM((tiles, modes, LANES), F32),
            pltpu.VMEM((tiles, modes, LANES), F32),
            pltpu.VMEM((tiles, modes, LANES), F32),
            pltpu.VMEM((tiles, modes, LANES), F32),
            pltpu.VMEM((n, 2 * modes + 16 * cut, LANES), BF16),
            pltpu.VMEM((n, 16 * (tiles - cut), LANES), BF16),
            dma((4, tiles)), dma((7,)), dma((7,)), dma((halves, n)), dma((halves, n)), dma((2, 2)),
            dma((2, n)), dma((2, n)),
        ],
        compiler_params=pltpu.CompilerParams(
            collective_id=0, has_side_effects=True, vmem_limit_bytes=60 * 1024 * 1024
        ),
    )(query, key, value, cot, taps, rates.T, weights.T)

    def stack(*shape):
        return pl.BlockSpec(shape, lambda j: (j, 0, 0))

    def wide(*shape):
        return pl.BlockSpec(shape, lambda j: (0, 0, j))

    tokens = pl.BlockSpec((length, LANES), lambda j: (0, j))
    big = shape((length, width), BF16)
    edges = pl.BlockSpec((1, 3, 8, LANES), lambda j: (j, 0, 0, 0))
    *grads, grad_res = pl.pallas_call(
        functools.partial(outputs_kernel, length, groups),
        grid=(tiles,),
        out_shape=(big, big, big, big, shape((3, 3, width), F32), shape((modes, groups), F32)),
        in_specs=[
            tokens, tokens, tokens, tokens, wide(3, 3, LANES), stack(1, length, LANES), stack(1, length, LANES),
            edges, edges, stack(1, 16, LANES),
            pl.BlockSpec((modes, LANES), lambda j: (0, 0)),
        ],
        out_specs=[tokens] * 4 + [wide(3, 3, LANES), pl.BlockSpec((modes, groups), lambda j: (0, 0))],
        scratch_shapes=[
            pltpu.VMEM((3, length + 16, LANES), F32),
            pltpu.VMEM((3, length + 8, LANES), F32),
        ],
        compiler_params=pltpu.CompilerParams(
            dimension_semantics=("arbitrary",), vmem_limit_bytes=60 * 1024 * 1024
        ),
    )(query, key, value, cot, taps, *middle)
    return (*grads, grad_res.T)


def solution(mesh):
    rows = P("ctx", "tp")
    n = mesh.shape["ctx"]
    return jax.shard_map(
        functools.partial(local, n),
        mesh=mesh,
        in_specs=(rows, rows, rows, rows, P(None, None, "tp"), P("tp", None), P("tp", None)),
        out_specs=(rows, rows, rows, rows, P(None, None, "tp"), P("tp", None)),
        check_vma=False,
    )
```

```python
import functools

import jax
import jax.numpy as jnp
from jax import lax
from jax.experimental import pallas as pl
from jax.experimental.pallas import tpu as pltpu
from jax.sharding import PartitionSpec as P

BLK = 128
LANES = 128
MEM = 16
HI = lax.Precision.HIGHEST
F32 = jnp.float32
BF16 = jnp.bfloat16
MESH = pl.DeviceIdType.MESH


def lane_iota(rows):
    return lax.broadcasted_iota(jnp.int32, (rows, LANES), 1)


def row_iota(rows):
    return lax.broadcasted_iota(jnp.int32, (rows, LANES), 0)


def turn(parts, piece):
    for d in (1, 2, 4):
        pick = (piece // d) % 2 == 1
        parts = [jnp.where(pick, parts[(g - d) % 8], parts[g]) for g in range(8)]
    return parts


def gather_groups(parts):
    piece = lane_iota(parts[0].shape[0]) // MEM
    parts = [pltpu.roll(p, MEM * b, 1) if b else p for b, p in enumerate(parts)]
    return turn([parts[-g % 8] for g in range(8)], piece)


def gather_blocks(parts):
    piece = lane_iota(parts[0].shape[0]) // MEM
    parts = turn([parts[-g % 8] for g in range(8)], piece)
    return [pltpu.roll(p, LANES - MEM * b, 1) if b else p for b, p in enumerate(parts)]


def split(value):
    high = value.astype(BF16)
    low = (value - high.astype(F32)).astype(BF16)
    return high, low


def dot(a, b, dims=((1,), (0,))):
    return lax.dot_general(a, b, (dims, ((), ())), preferred_element_type=F32)


def column(table, g):
    return jnp.broadcast_to(table[:, MEM * g : MEM * g + 1], table.shape)


def filters_kernel(
    n, tiles, halves, length, modes,
    query, key, value, cot, taps, rates, weights,
    long_out, back_out, prior_out, next_out, taps_out, res_out,
    inb, uf, xs, gs, tf, tb, sf, sb, fs, gb, st, rs, halo, after, r3, w3, gacc, yv, zv, stage, tsum, rc, rn, wn, sout, gin, *rest,
):
    early, late = rest[0:2]
    in_sem, hs_sem, hr_sem, ss_sem, sr_sem, out_sem, ts_sem, tr_sem = rest[2:]
    me = lax.axis_index("ctx")
    per = tiles // halves
    barrier = pltpu.get_barrier_semaphore()
    for d in range(1, n):
        pl.semaphore_signal(barrier, inc=1, device_id={"ctx": lax.rem(me + d, n)}, device_id_type=MESH)

    streams = (query, key, value, cot)

    def fetch(i, j):
        return pltpu.make_async_copy(
            streams[i].at[:, pl.ds(pl.multiple_of(j * LANES, LANES), LANES)], inb.at[i, j], in_sem.at[i, j]
        )

    for j in range(tiles):
        for i in range(4):
            fetch(i, j).start()

    def exact(a, b, dims):
        return lax.dot_general(a, b, (dims, ((), ())), precision=HI, preferred_element_type=F32)

    repeat = (lane_iota(modes) % modes == row_iota(modes)).astype(F32)
    for j in range(tiles):
        group = (lane_iota(8 * tiles) // MEM + 8 * j == row_iota(8 * tiles)).astype(F32)
        rn[j] = exact(rates[...], group, ((1,), (0,)))
        wn[j] = exact(weights[...], group, ((1,), (0,)))
    r3[...] = exact(rates[...], repeat, ((0,), (0,)))
    w3[...] = exact(weights[...], repeat, ((0,), (0,)))

    t_row = row_iota(BLK).astype(F32)
    lane_f = lane_iota(modes).astype(F32)
    lane_b = lane_iota(BLK)
    causal = row_iota(BLK) >= lane_iota(BLK)
    anti = row_iota(BLK) <= lane_iota(BLK)

    def build(j, _):
        rn_j = rn[j]
        for g in range(8):
            at = 8 * j + g
            r_row = r3[pl.ds(at, 1), :]
            w_row = w3[pl.ds(at, 1), :]
            r_col = column(rn_j, g)
            rc[at] = r_col
            pad = jnp.zeros((LANES - 3 * modes, LANES), BF16)
            for ref, reach, peer, mask in (
                (tf, t_row + 1.0, lane_f + 1.0, causal),
                (tb, (BLK - 1.0) - t_row, (BLK - 1.0) - lane_f, anti),
            ):
                high, low = split(w_row * jnp.exp(-r_row * reach))
                zero = jnp.zeros_like(high)
                left = jnp.where(lane_b < 2 * modes, high, jnp.where(lane_b < 3 * modes, low, zero))
                v_high, v_low = split(jnp.exp(r_col * peer))
                right = jnp.concatenate([v_high, v_low, v_high, pad], axis=0)
                table = dot(left, right)
                ref[at, :, 0:BLK] = jnp.where(mask, table, 0.0).astype(BF16)
                ref[at, :, BLK : 2 * BLK] = left
        return 0

    lax.fori_loop(0, tiles // 2, build, 0, unroll=2)
    pl.semaphore_wait(barrier, n - 1)

    def behind(i):
        return pltpu.make_async_remote_copy(
            src_ref=streams[i].at[pl.ds(length - 16, 16), :], dst_ref=halo.at[i],
            send_sem=hs_sem.at[i], recv_sem=hr_sem.at[i],
            device_id={"ctx": lax.rem(me + 1, n)}, device_id_type=MESH,
        )

    def ahead(i):
        return pltpu.make_async_remote_copy(
            src_ref=streams[i].at[pl.ds(0, 16), :], dst_ref=after.at[i],
            send_sem=hs_sem.at[3 + i], recv_sem=hr_sem.at[3 + i],
            device_id={"ctx": lax.rem(me + n - 1, n)}, device_id_type=MESH,
        )

    for i in range(3):
        behind(i).start()
    for i in range(4):
        ahead(i).start()

    lax.fori_loop(tiles // 2, tiles, build, 0, unroll=2)

    def arrive(j, _):
        for i in range(4):
            fetch(i, j).wait()

        def widen(c, _):
            for i in range(3):
                rows = pl.ds(pl.multiple_of(c * 64, 64), 64)
                uf[j, i, pl.ds(pl.multiple_of(c * 64 + 8, 8), 64), :] = inb[i, j, rows, :].astype(F32)
            return 0

        lax.fori_loop(0, length // 64, widen, 0, unroll=4)
        return 0

    lax.fori_loop(0, tiles, arrive, 0)
    def gate_of(j):
        lanes = pl.ds(pl.multiple_of(j * LANES, LANES), LANES)
        tap = [[taps[i, l : l + 1, lanes] for l in range(3)] for i in range(3)]

        def gate(c, _):
            s0 = pl.multiple_of(c * 16, 16)
            forward, backward = [], []
            for b in range(8):
                base = pl.multiple_of(b * BLK + s0, 16)
                short = []
                for i in range(3):
                    view = uf.at[j, i, pl.ds(base, 24), :]
                    total = tap[i][0] * view[8:24, :] + tap[i][1] * view[7:23, :] + tap[i][2] * view[6:22, :]
                    short.append(total)
                forward.append(short[1] * short[2])
                backward.append(inb[3, j, pl.ds(base, 16), :].astype(F32) * short[0])
            for ref, parts in ((xs, forward), (gs, backward)):
                for g, part in enumerate(gather_groups(parts)):
                    ref[8 * j + g, pl.ds(s0, 16), :] = part.astype(BF16)
            return 0

        return gate

    def gates(j, _):
        lax.fori_loop(1, BLK // 16, gate_of(j), 0, unroll=7)
        return 0

    lax.fori_loop(0, tiles, gates, 0)
    for i in range(3):
        behind(i).wait()
    for i in range(4):
        ahead(i).wait()

    first = (me == 0)
    last = (me == n - 1)
    lane16 = lane_iota(modes)

    def phase1(j, _):
        lanes = pl.ds(pl.multiple_of(j * LANES, LANES), LANES)
        for i in range(3):
            prior = halo[i, :, lanes].astype(F32)[8:16]
            prior = jnp.where(first, 0.0, prior)
            uf[j, i, 0:8, :] = prior
            prior_out[j, i] = prior
            uf[j, i, 8 + length : 16 + length, :] = jnp.where(last, 0.0, after[i, :, lanes].astype(F32)[0:8])

        lax.fori_loop(0, 1, gate_of(j), 0)

        step = jnp.exp(-rn[j] * float(BLK))
        ends, starts = [], []
        for g in range(8):
            at = 8 * j + g
            r_col = rc[at]
            absorb = jnp.concatenate(split(jnp.exp(-r_col * ((BLK - 1.0) - lane_f))), axis=0)
            both = dot(absorb, xs[at])
            ends.append(both[0:modes] + both[modes : 2 * modes])
            emit = jnp.concatenate(split(jnp.exp(-r_col * (lane_f + 1.0))), axis=0)
            both = dot(emit, gs[at])
            starts.append(both[0:modes] + both[modes : 2 * modes])
        ends, starts = gather_blocks(ends), gather_blocks(starts)
        ahead_state = back_state = jnp.zeros((modes, LANES), F32)
        for b in range(8):
            fs[0, j, b] = ahead_state
            ahead_state = step * ahead_state + ends[b]
            gb[j, b] = starts[b]
        for b in range(7, -1, -1):
            fs[1, j, b] = back_state
            back_state = step * back_state + starts[b]
        st[j // per, 0, j % per] = ahead_state.astype(BF16)
        st[j // per, 1, j % per] = back_state.astype(BF16)
        return 0

    def send(h, d):
        return pltpu.make_async_remote_copy(
            src_ref=st.at[h, (me + d) // n], dst_ref=rs.at[h, d],
            send_sem=ss_sem.at[h, d], recv_sem=sr_sem.at[h, d],
            device_id={"ctx": lax.rem(me + d, n)}, device_id_type=MESH,
        )

    for h in range(halves):
        lax.fori_loop(h * per, (h + 1) * per, phase1, 0)
        for d in range(1, n):
            send(h, d).start()

    gacc[...] = jnp.zeros_like(gacc)

    def within(j, _):
        rn_j = rn[j]
        total = gacc[...]
        turned = [gs[8 * j + g].astype(F32).T.astype(BF16) for g in range(8)]
        pairs = [dot(xs[8 * j + g], turned[g]) for g in range(8)]
        pairs = [jnp.where(anti, p, 0.0).astype(BF16) for p in pairs]
        for g in range(8):
            r_col = rc[8 * j + g]
            rise = jnp.concatenate(split(jnp.exp(r_col * lane_f)), axis=0)
            both = dot(rise, pairs[g])
            terms = (both[0:modes] + both[modes : 2 * modes]) * jnp.exp(-r_col * lane_f)
            total = jnp.where(lane16 == 8 * j + g, total + jnp.sum(terms, axis=1, keepdims=True), total)
        gacc[...] = total
        return 0

    lax.fori_loop(0, tiles, within, 0, unroll=2)

    def combine(j, h):
        jj = j - h * per
        rn_j = rn[j]
        whole = jnp.exp(-rn_j * float(length))
        into = jnp.zeros((modes, LANES), F32)
        back = jnp.zeros((modes, LANES), F32)
        for e in range(n - 1, 0, -1):
            into = whole * into + jnp.where(e <= me, rs[h, e, jj].astype(F32), 0.0)
            back = whole * back + jnp.where(e <= n - 1 - me, rs[h, n - e, jj].astype(F32), 0.0)
        sout[j] = whole * into + st[h, 0, jj].astype(F32)
        gin[j] = back
        step = jnp.exp(-rn_j * float(BLK))
        reach_in, reach_back = into, back
        before, behind_ = [None] * 8, [None] * 8
        for b in range(8):
            before[b] = fs[0, j, b] + reach_in
            behind_[7 - b] = fs[1, j, 7 - b] + reach_back
            reach_in = step * reach_in
            reach_back = step * reach_back
        terms = gb[j, 0] * before[0]
        for b in range(1, 8):
            terms = terms + gb[j, b] * before[b]
        group = (row_iota(LANES) // MEM + 8 * j == lane_iota(LANES)).astype(F32)
        gacc[...] += exact(terms, group, ((1,), (0,)))
        for ref, blocks in ((sf, before), (sb, behind_)):
            for g, state in enumerate(gather_groups(blocks)):
                high, low = split(state)
                ref[8 * j + g] = jnp.concatenate([high, low, high], axis=0)
        return h


    def put(i, j, slot):
        return pltpu.make_async_copy(stage.at[slot, i], (long_out, back_out)[i].at[j], out_sem.at[slot, i])

    pad = jnp.zeros((BLK - 3 * modes, LANES), BF16)

    def phase2(j, _):
        lanes = pl.ds(pl.multiple_of(j * LANES, LANES), LANES)
        slot = j % 2

        @pl.when(j >= 2)
        def _():
            for i in range(2):
                put(i, j - 2, slot).wait()

        for g in range(8):
            at = 8 * j + g
            yv[g] = dot(tf[at], jnp.concatenate([xs[at], sf[at], pad], axis=0))
            zv[g] = dot(tb[at], jnp.concatenate([gs[at], sb[at], pad], axis=0))
        tap = [[taps[i, l : l + 1, lanes] for l in range(3)] for i in range(3)]

        def finish(c, sums):
            s0 = pl.multiple_of(c * 16, 16)
            rows = pl.ds(s0, 16)
            longs = gather_blocks([yv[g, rows, :] for g in range(8)])
            backs = gather_blocks([zv[g, rows, :] for g in range(8)])
            sums = list(sums)
            for b in range(8):
                base = pl.multiple_of(b * BLK + s0, 16)
                short, windows = [], []
                for i in range(3):
                    view = uf.at[j, i, pl.ds(base, 24), :]
                    win = [view[8 - l : 24 - l, :] for l in range(3)]
                    windows.append(win)
                    if i:
                        short.append(tap[i][0] * win[0] + tap[i][1] * win[1] + tap[i][2] * win[2])
                grads = (
                    inb[3, j, pl.ds(base, 16), :].astype(F32) * longs[b],
                    backs[b] * short[1],
                    backs[b] * short[0],
                )
                for i in range(3):
                    for l in range(3):
                        term = grads[i] * windows[i][l]
                        sums[3 * i + l] = sums[3 * i + l] + (term[0:8] + term[8:16])
            for b in range(8):
                rows = pl.ds(pl.multiple_of(b * BLK + s0, 16), 16)
                stage[slot, 0, rows, :] = longs[b].astype(BF16)
                stage[slot, 1, rows, :] = backs[b].astype(BF16)
            return tuple(sums)

        sums = lax.fori_loop(0, BLK // 16, finish, (jnp.zeros((8, LANES), F32),) * 9, unroll=4)
        for at in range(9):
            tsum[j, at : at + 1, :] = jnp.sum(sums[at], axis=0, keepdims=True)
        tsum[j, 9:16, :] = jnp.zeros((7, LANES), F32)
        for i in range(2):
            put(i, j, slot).start()
        return 0

    def give(m, d):
        box = (early, late)[m]
        return pltpu.make_async_remote_copy(
            src_ref=box.at[me], dst_ref=box.at[me], send_sem=ts_sem.at[m, d], recv_sem=tr_sem.at[m, d],
            device_id={"ctx": lax.rem(me + d, n)}, device_id_type=MESH,
        )

    def absorb_half(h):
        for d in range(1, n):
            send(h, d).wait()
        lax.fori_loop(h * per, (h + 1) * per, combine, h)

    cut = max(0, tiles - 2)
    absorb_half(0)
    if halves == 2:
        lax.fori_loop(0, min(per, cut), phase2, 0)
        absorb_half(1)
    for m, (lo, hi) in enumerate(((0, cut), (cut, tiles))):
        lax.fori_loop(min(per, cut) if m == 0 else lo, hi, phase2, 0)
        box = (early, late)[m]
        base = 0
        if m == 0:
            high, low = split(gacc[...])
            box[me, 0:modes, :] = high
            box[me, modes : 2 * modes, :] = low
            base = 2 * modes
        for j in range(lo, hi):
            box[me, base + 16 * (j - lo) : base + 16 * (j - lo + 1), :] = tsum[j].astype(BF16)
        for d in range(1, n):
            give(m, d).start()
    def follow(j, _):
        lanes = pl.ds(pl.multiple_of(j * LANES, LANES), LANES)
        tap = [[taps[i, l : l + 1, lanes] for l in range(3)] for i in range(3)]

        rn_j, wn_j = rn[j], wn[j]
        one = jnp.exp(rn_j)
        less = jnp.exp(-rn_j)

        def over(x):
            return jnp.sum(x, axis=0, keepdims=True)

        short = []
        for i in range(3):
            view = uf.at[j, i, length : length + 16, :]
            short.append(tap[i][0] * view[8:16, :] + tap[i][1] * view[7:15, :] + tap[i][2] * view[6:14, :])
        cot_next = jnp.where(last, 0.0, after[3, :, lanes].astype(F32)[0:8])
        x_next = (short[1] * short[2]).astype(BF16).astype(F32)[0:2]
        g_next = (cot_next * short[0]).astype(BF16).astype(F32)[0:1]
        h0 = over(wn_j)
        h1 = over(wn_j * less)
        long0 = over(wn_j * less * sout[j]) + h0 * x_next[0:1]
        long1 = over(wn_j * less * less * sout[j]) + h1 * x_next[0:1] + h0 * x_next[1:2]
        gg0 = over(wn_j * one * gin[j])
        gg1 = over(wn_j * one * one * gin[j]) - over(wn_j * one) * g_next
        row8 = row_iota(8)
        long_next = jnp.where(row8 == 0, long0, jnp.where(row8 == 1, long1, 0.0))
        gg_next = jnp.where(row8 == 0, gg0, jnp.where(row8 == 1, gg1, 0.0))
        next_out[j, 0] = cot_next * long_next
        next_out[j, 1] = gg_next * short[2]
        next_out[j, 2] = gg_next * short[1]
        return 0

    lax.fori_loop(0, tiles, follow, 0)
    for j in range(max(0, tiles - 2), tiles):
        for i in range(2):
            put(i, j, j % 2).wait()
    for m, (lo, hi) in enumerate(((0, cut), (cut, tiles))):
        for d in range(1, n):
            give(m, d).wait()
        box = (early, late)[m]
        total = box[0].astype(F32)
        for s in range(1, n):
            total = total + box[s].astype(F32)
        base = 0
        if m == 0:
            res_out[...] = total[0:modes] + total[modes : 2 * modes]
            base = 2 * modes
        for j in range(lo, hi):
            taps_out[j] = total[base + 16 * (j - lo) : base + 16 * (j - lo + 1)]


def outputs_kernel(
    length, groups,
    query, key, value, cot, taps, long_low, back_low, prior, following, taps_sum, res_sum,
    mixed, grad_q, grad_k, grad_v, grad_taps, grad_res,
    uf, ef,
):
    for i in range(3):
        uf[i, 0:8, :] = prior[0, i]
        ef[i, length : length + 8, :] = following[0, i]
    streams = (query, key, value)

    def widen(c, _):
        for i in range(3):
            rows = pl.ds(pl.multiple_of(c * 64, 64), 64)
            uf[i, pl.ds(pl.multiple_of(c * 64 + 8, 8), 64), :] = streams[i][rows, :].astype(F32)
        return 0

    lax.fori_loop(0, length // 64, widen, 0, unroll=4)
    tap = [[taps[i, l : l + 1, :] for l in range(3)] for i in range(3)]

    size = 64

    def spread(c, _):
        base = pl.multiple_of(length - size - c * size, size)
        rows = pl.ds(base, size)
        short = []
        for i in range(3):
            view = uf.at[i, pl.ds(base, size + 8), :]
            win = [view[8 - l : 8 + size - l, :] for l in range(3)]
            short.append(tap[i][0] * win[0] + tap[i][1] * win[1] + tap[i][2] * win[2])
        long_here = long_low[0, rows, :].astype(F32)
        back_here = back_low[0, rows, :].astype(F32)
        mixed[rows, :] = (short[0] * long_here).astype(BF16)
        grads = (cot[rows, :].astype(F32) * long_here, back_here * short[2], back_here * short[1])
        for i in range(3):
            ef[i, rows, :] = grads[i]
            view = ef.at[i, pl.ds(base, size + 8), :]
            total = tap[i][0] * grads[i] + tap[i][1] * view[1 : 1 + size, :] + tap[i][2] * view[2 : 2 + size, :]
            (grad_q, grad_k, grad_v)[i][rows, :] = total.astype(BF16)
        return 0

    lax.fori_loop(0, length // size, spread, 0, unroll=4)
    for i in range(3):
        grad_taps[i] = taps_sum[0, 3 * i : 3 * i + 3, :]
    grad_res[...] = res_sum[:, 0:groups]


def local(n, query, key, value, cot, taps, weights, rates):
    length, width = query.shape
    groups, modes = rates.shape
    tiles = width // LANES
    halves = 2 if tiles % 2 == 0 else 1
    per = tiles // halves
    cut = max(0, tiles - 2)
    hbm = pl.BlockSpec(memory_space=pl.ANY)
    vmem = pl.BlockSpec(memory_space=pltpu.VMEM)
    dma = pltpu.SemaphoreType.DMA
    shape = jax.ShapeDtypeStruct
    edge = shape((tiles, 3, 8, LANES), F32)
    tokens3 = shape((tiles, length, LANES), BF16)
    middle = pl.pallas_call(
        functools.partial(filters_kernel, n, tiles, halves, length, modes),
        out_shape=(
            tokens3, tokens3, edge, edge, shape((tiles, 16, LANES), F32), shape((modes, LANES), F32),
        ),
        in_specs=[hbm] * 4 + [vmem] * 3,
        out_specs=[hbm] * 2 + [vmem] * 4,
        scratch_shapes=[
            pltpu.VMEM((4, tiles, length, LANES), BF16),
            pltpu.VMEM((tiles, 3, length + 16, LANES), F32),
            pltpu.VMEM((groups, BLK, LANES), BF16),
            pltpu.VMEM((groups, BLK, LANES), BF16),
            pltpu.VMEM((groups, BLK, 2 * LANES), BF16),
            pltpu.VMEM((groups, BLK, 2 * LANES), BF16),
            pltpu.VMEM((groups, 3 * modes, LANES), BF16),
            pltpu.VMEM((groups, 3 * modes, LANES), BF16),
            pltpu.VMEM((2, tiles, 8, modes, LANES), F32),
            pltpu.VMEM((tiles, 8, modes, LANES), F32),
            pltpu.VMEM((halves, 2, per, modes, LANES), BF16),
            pltpu.VMEM((halves, n, per, modes, LANES), BF16),
            pltpu.VMEM((3, 16, width), BF16),
            pltpu.VMEM((4, 16, width), BF16),
            pltpu.VMEM((groups, LANES), F32),
            pltpu.VMEM((groups, LANES), F32),
            pltpu.VMEM((modes, LANES), F32),
            pltpu.VMEM((8, BLK, LANES), F32),
            pltpu.VMEM((8, BLK, LANES), F32),
            pltpu.VMEM((2, 2, length, LANES), BF16),
            pltpu.VMEM((tiles, 16, LANES), F32),
            pltpu.VMEM((groups, modes, LANES), F32),
            pltpu.VMEM((tiles, modes, LANES), F32),
            pltpu.VMEM((tiles, modes, LANES), F32),
            pltpu.VMEM((tiles, modes, LANES), F32),
            pltpu.VMEM((tiles, modes, LANES), F32),
            pltpu.VMEM((n, 2 * modes + 16 * cut, LANES), BF16),
            pltpu.VMEM((n, 16 * (tiles - cut), LANES), BF16),
            dma((4, tiles)), dma((7,)), dma((7,)), dma((halves, n)), dma((halves, n)), dma((2, 2)),
            dma((2, n)), dma((2, n)),
        ],
        compiler_params=pltpu.CompilerParams(
            collective_id=0, has_side_effects=True, vmem_limit_bytes=60 * 1024 * 1024
        ),
    )(query, key, value, cot, taps, rates.T, weights.T)

    def stack(*shape):
        return pl.BlockSpec(shape, lambda j: (j, 0, 0))

    def wide(*shape):
        return pl.BlockSpec(shape, lambda j: (0, 0, j))

    tokens = pl.BlockSpec((length, LANES), lambda j: (0, j))
    big = shape((length, width), BF16)
    edges = pl.BlockSpec((1, 3, 8, LANES), lambda j: (j, 0, 0, 0))
    *grads, grad_res = pl.pallas_call(
        functools.partial(outputs_kernel, length, groups),
        grid=(tiles,),
        out_shape=(big, big, big, big, shape((3, 3, width), F32), shape((modes, groups), F32)),
        in_specs=[
            tokens, tokens, tokens, tokens, wide(3, 3, LANES), stack(1, length, LANES), stack(1, length, LANES),
            edges, edges, stack(1, 16, LANES),
            pl.BlockSpec((modes, LANES), lambda j: (0, 0)),
        ],
        out_specs=[tokens] * 4 + [wide(3, 3, LANES), pl.BlockSpec((modes, groups), lambda j: (0, 0))],
        scratch_shapes=[
            pltpu.VMEM((3, length + 16, LANES), F32),
            pltpu.VMEM((3, length + 8, LANES), F32),
        ],
        compiler_params=pltpu.CompilerParams(
            dimension_semantics=("arbitrary",), vmem_limit_bytes=60 * 1024 * 1024
        ),
    )(query, key, value, cot, taps, *middle)
    return (*grads, grad_res.T)


def solution(mesh):
    rows = P("ctx", "tp")
    n = mesh.shape["ctx"]
    return jax.shard_map(
        functools.partial(local, n),
        mesh=mesh,
        in_specs=(rows, rows, rows, rows, P(None, None, "tp"), P("tp", None), P("tp", None)),
        out_specs=(rows, rows, rows, rows, P(None, None, "tp"), P("tp", None)),
        check_vma=False,
    )
```
